512 devices in a mesh: gx: 8 (over z), gy: 4 (over x), gz: 16 (over y, core).
Axes of the slice: x: 4, y: 8, z: 8, core: 2. Of those that a mesh axis runs over, the one named last changes fastest.
Arguments:
- positions: float32 [8, 4, 16, 3, 768], P('gx', 'gy', 'gz'), may hold values from 0 to 1
- smoothing: float32 [8, 4, 16, 768], P('gx', 'gy', 'gz'), may hold values from 0.49 to 0.5
- masses: float32 [8, 4, 16, 768], P('gx', 'gy', 'gz'), may hold values from 0.0006510417 to 0.0026041667
- entropy: float32 [8, 4, 16, 768], P('gx', 'gy', 'gz'), may hold values from 0.5 to 2
- old_density: float32 [8, 4, 16, 768], P('gx', 'gy', 'gz'), may hold values from 0.5 to 2
- active: int32 [8, 4, 16, 768], P('gx', 'gy', 'gz'), may hold values 0 or 1
Outputs:
- density: float32 [8, 4, 16, 768], P('gx', 'gy', 'gz')
- acceleration: float32 [8, 4, 16, 3, 768], P('gx', 'gy', 'gz')
The draws below stay inside these ranges and needn't reach their ends.
All inputs are finite; a program needn't handle non-finite values. No bound on the sum of `active` on one device may be relied on, other than what follows from the above.
Results may differ from the reference program's by a relative error of at most 0.0001.
Values sent between devices are 32-bit elements; how exact they have to be, the bound alone decides.
No kernel may reach another device: no remote copies, remote signals or barrier semaphores. Data moves between devices by JAX's collectives and lax.ppermute only.
A program may use at most 64 MiB of HBM per device.

```python
import math
import jax
import jax.numpy as jnp
from jax import lax

PART_CELL = 768
NX = 8
NY = 4
NZ = 16


def touch_ends(drawn, key, smallest, largest):
    dims = drawn.shape
    place = [jax.random.randint(jax.random.fold_in(key, axis), (), 0, dims[axis]) for axis in range(len(dims))]
    drawn = drawn.at[tuple(place)].set(smallest)
    longest = dims.index(max(dims))
    place[longest] = (place[longest] + 1) % dims[longest]
    return drawn.at[tuple(place)].set(largest)


def block_scale(own_key, shape, shards, least, high):
    def one(dim, shards_of):
        heights = jax.random.uniform(jax.random.fold_in(jax.random.fold_in(own_key, 6), dim), (shards_of,), jnp.float32, least / len(shards), high / len(shards))
        return jnp.repeat(jnp.exp(heights), shape[dim] // shards_of).reshape((-1,) + (1,) * (len(shape) - dim - 1))

    factor_of = one(*shards[0])
    for cut in shards[1:]:
        factor_of = factor_of * one(*cut)
    return factor_of


def setup_inputs(seed: int = 0) -> dict:
    key_of = jax.random.split(jax.random.key(seed), 7)
    return {
        "positions": jnp.clip(1.0 * jax.random.uniform(key_of[0], (NX, NY, NZ, 3, PART_CELL), jnp.float32) ** block_scale(key_of[0], (NX, NY, NZ, 3, PART_CELL), ((0, 8), (1, 4), (2, 16)), -0.2, 0.2), 0.0, 1.0),
        "smoothing": jnp.clip(0.49 + 0.00999999 * jax.random.uniform(key_of[1], (NX, NY, NZ, PART_CELL), jnp.float32) ** block_scale(key_of[1], (NX, NY, NZ, PART_CELL), ((0, 8), (1, 4), (2, 16)), -0.2, 0.2), 0.49, 0.5),
        "masses": jnp.clip(jnp.exp(math.log(0.0026041667) - 1.3862944 * jax.random.uniform(key_of[2], (NX, NY, NZ, PART_CELL), jnp.float32) ** block_scale(key_of[2], (NX, NY, NZ, PART_CELL), ((0, 8), (1, 4), (2, 16)), -0.2, 0.2)), 0.0006510417, 0.0026041667),
        "entropy": jnp.clip(jnp.exp(math.log(2.0) - 1.3862944 * jax.random.uniform(key_of[3], (NX, NY, NZ, PART_CELL), jnp.float32) ** block_scale(key_of[3], (NX, NY, NZ, PART_CELL), ((0, 8), (1, 4), (2, 16)), -0.2, 0.2)), 0.5, 2.0),
        "old_density": jnp.clip(jnp.exp(math.log(2.0) - 1.3862944 * jax.random.uniform(key_of[4], (NX, NY, NZ, PART_CELL), jnp.float32) ** block_scale(key_of[4], (NX, NY, NZ, PART_CELL), ((0, 8), (1, 4), (2, 16)), -0.2, 0.2)), 0.5, 2.0),
        "active": touch_ends((jax.random.randint(key_of[5], (NX, NY, NZ, PART_CELL), 0, 2) < 1).astype(jnp.int32), jax.random.fold_in(key_of[5], 1), 0, 1),
    }


KW = 21.0 / (2.0 * math.pi)
KG = 210.0 / math.pi

def offsets_table():
    k = jnp.arange(27, dtype=jnp.int32)
    return jnp.stack([k // 9 - 1, k // 3 % 3 - 1, k % 3 - 1], axis=1).astype(jnp.float32)

def separation(own_pos, other_pos, shift):
    return own_pos[:, :, None] - (other_pos[:, None, :] + shift[:, None, None])

def density_term(own_pos, own_h, other_pos, other_mass, shift):
    sep = separation(own_pos, other_pos, shift)
    dist = jnp.sqrt(lax.optimization_barrier(jnp.sum(sep * sep, axis=0)))
    ratio = dist / own_h[:, None]
    rest = jnp.maximum(1.0 - ratio, 0.0)
    weight = KW * rest ** 4 * (1.0 + 4.0 * ratio) / own_h[:, None] ** 3
    return lax.optimization_barrier(jnp.sum(weight * other_mass[None, :], axis=1))

def force_term(own_pos, own_h, own_pr, other_pos, other_h, other_mass, other_pr, shift):
    sep = separation(own_pos, other_pos, shift)
    dist = jnp.sqrt(lax.optimization_barrier(jnp.sum(sep * sep, axis=0)))
    rest_own = jnp.maximum(1.0 - dist / own_h[:, None], 0.0)
    rest_far = jnp.maximum(1.0 - dist / other_h[None, :], 0.0)
    coef = KG * other_mass[None, :] * (own_pr[:, None] * rest_own ** 3 / own_h[:, None] ** 5 + other_pr[None, :] * rest_far ** 3 / other_h[None, :] ** 5)
    return lax.optimization_barrier(jnp.sum(coef[None] * sep, axis=2))

def cell_density(own, neigh):

    def step(total, item):
        block, shift = item
        return (total + density_term(own[0:3], own[3], block[0:3], block[4], shift), None)
    start = jnp.zeros((own.shape[1],), jnp.float32)
    total, _ = lax.scan(step, start, (neigh, offsets_table()))
    return total

def cell_force(own, own_pr, neigh, neigh_pr):

    def step(total, item):
        block, block_pr, shift = item
        return (total + force_term(own[0:3], own[3], own_pr, block[0:3], block[3], block[4], block_pr, shift), None)
    start = jnp.zeros((3, own.shape[1]), jnp.float32)
    total, _ = lax.scan(step, start, (neigh, neigh_pr, offsets_table()))
    return total

def neighbours(field):
    stacked = []
    for ddx in (-1, 0, 1):
        for ddy in (-1, 0, 1):
            for ddz in (-1, 0, 1):
                stacked.append(jnp.roll(field, (-ddx, -ddy, -ddz), (0, 1, 2)))
    return jnp.stack(stacked, axis=0)

def reference(positions, smoothing, masses, entropy, old_density, active):
    cells = NX * NY * NZ
    state = jnp.concatenate([positions, smoothing[:, :, :, None, :], masses[:, :, :, None, :], entropy[:, :, :, None, :]], axis=3)
    flat = state.reshape(cells, 6, PART_CELL)
    beside_all = neighbours(state).reshape(27, cells, 6, PART_CELL).transpose(1, 0, 2, 3)
    rho_new = lax.map(lambda item: cell_density(item[0], item[1]), (flat, beside_all))
    rho_new = rho_new.reshape(NX, NY, NZ, PART_CELL)
    live = active == 1
    density = jnp.where(live, rho_new, old_density)
    pres = entropy * jnp.power(density, -1.0 / 3.0)
    around_pr = neighbours(pres).reshape(27, cells, PART_CELL).transpose(1, 0, 2)
    accel = lax.map(lambda item: cell_force(item[0], item[1], item[2], item[3]), (flat, pres.reshape(cells, PART_CELL), beside_all, around_pr))
    accel = accel.reshape(NX, NY, NZ, 3, PART_CELL)
    accel = jnp.where(live[:, :, :, None, :], accel, jnp.float32(0.0))
    return (density, accel)
```

```python
import itertools
import math

import jax
import jax.numpy as jnp
from jax import lax
from jax.experimental import pallas as pl
from jax.experimental.pallas import tpu as pltpu
from jax.sharding import PartitionSpec as P

KW = 21.0 / (2.0 * math.pi)
KG = 210.0 / math.pi
LANES = 128
COUNT = 768
BLOCKS = COUNT // LANES
FAR = 1.0e4
IROWS = 16
OFFSETS = [dx * 16 + dy * 4 + dz for dx, dy, dz in itertools.product((-1, 0, 1), repeat=3)]
ROW_Q = 6
ROW_META = 7


def cbrt(x):
    return jnp.exp(jnp.log(x) * (1.0 / 3.0))


def inv_cbrt(x):
    return jnp.exp(jnp.log(x) * (-1.0 / 3.0))


def split3(rows):
    hi = rows.astype(jnp.bfloat16).astype(jnp.float32)
    rest = rows - hi
    mid = rest.astype(jnp.bfloat16).astype(jnp.float32)
    low = rest - mid
    return jnp.concatenate([hi, mid, low, jnp.zeros_like(hi)], axis=0).astype(jnp.bfloat16)


def join3(parts):
    return parts[0:8] + parts[8:16] + parts[16:24]


def one_hot_of(rank):
    place = lax.broadcasted_iota(jnp.int32, (COUNT, COUNT), 0)
    return (place == rank).astype(jnp.float32).astype(jnp.bfloat16)


def sort_kernel(pos_ref, h_ref, m_ref, a_ref, old_ref, act_ref, unit_ref, rank_ref):
    x, y, z = pos_ref[0:1], pos_ref[1:2], pos_ref[2:3]
    ih = 1.0 / h_ref[...]
    ih2 = ih * ih
    mass = m_ref[...]
    b = mass * a_ref[...] * (ih2 * ih2 * ih)
    q = b * inv_cbrt(old_ref[...])
    one, zero = jnp.int32(1), jnp.int32(0)
    key = (
        jnp.where(x >= 0.5, 8 * one, zero)
        + jnp.where(y >= 0.5, 4 * one, zero)
        + jnp.where(z >= 0.5, 2 * one, zero)
        + jnp.where(act_ref[...] == 1, zero, one)
    )
    kind = lax.broadcasted_iota(jnp.int32, (16, COUNT), 0)
    hot = (kind == key).astype(jnp.float32)
    blocks = jnp.concatenate([hot[:, k * LANES : (k + 1) * LANES] for k in range(BLOCKS)], axis=0)
    before = lax.broadcasted_iota(jnp.int32, (LANES, LANES), 0)
    after = lax.broadcasted_iota(jnp.int32, (LANES, LANES), 1)
    upper = (before < after).astype(jnp.float32).astype(jnp.bfloat16)
    prefix = jnp.dot(blocks.astype(jnp.bfloat16), upper, preferred_element_type=jnp.float32)
    sums = [jnp.sum(hot[:, k * LANES : (k + 1) * LANES], axis=1, keepdims=True) for k in range(BLOCKS)]
    running = jnp.zeros((16, 1), jnp.float32)
    carried = []
    for k in range(BLOCKS):
        carried.append(prefix[16 * k : 16 * (k + 1)] + running)
        running = running + sums[k]
    total = jnp.broadcast_to(running, (16, LANES))
    start = jnp.zeros((16, LANES), jnp.float32)
    row = lax.broadcasted_iota(jnp.int32, (16, LANES), 0)
    for k in range(15):
        start = start + jnp.where(row > k, total[k : k + 1], 0.0)
    rank = jnp.concatenate(
        [
            jnp.sum(
                hot[:, k * LANES : (k + 1) * LANES] * (carried[k] + start), axis=0, keepdims=True
            )
            for k in range(BLOCKS)
        ],
        axis=1,
    ).astype(jnp.int32)
    rank_ref[...] = rank
    rows = jnp.concatenate([x, y, z, ih, mass, b, q, jnp.zeros_like(q)], axis=0)
    moved = lax.dot_general(
        split3(rows), one_hot_of(rank), (((1,), (1,)), ((), ())), preferred_element_type=jnp.float32
    )
    moved = join3(moved)
    lane = lax.broadcasted_iota(jnp.int32, (16, LANES), 1)
    even = (row & 1) == 0
    octant = row >> 1
    counts = (
        jnp.where((lane == octant) & even, start, 0.0)
        + jnp.where(lane == octant + 8, total, 0.0)
        + jnp.where((lane == octant + 16) & even, total, 0.0)
    )
    counts = jnp.sum(counts, axis=0, keepdims=True)
    which = lax.broadcasted_iota(jnp.int32, (8, LANES), 0)
    for k in range(BLOCKS):
        unit_ref[k] = jnp.where(which == ROW_META, counts, moved[:, k * LANES : (k + 1) * LANES])


def octant_place(gx, gy, gz, shift):
    side = 2 + shift
    ex, ey, ez = gx + shift, gy + shift, gz + shift
    cx, cy, cz = ex // 2, ey // 2, ez // 2
    cell = (cx * side + cy) * side + cz
    octant = (ex % 2) * 4 + (ey % 2) * 2 + ez % 2
    return cell, octant, (cx, cy, cz)


def whole(value):
    return value.astype(jnp.int32)


def taken(units, cell, first, count, moves, force):
    block = jnp.minimum(first // LANES, BLOCKS - 1)
    later = jnp.minimum(block + 1, BLOCKS - 1)
    turn = first % LANES
    back = (LANES - turn) & (LANES - 1)
    lane = lax.broadcasted_iota(jnp.int32, (8, LANES), 1)
    chunk = jnp.where(
        lane < LANES - turn,
        pltpu.roll(units[cell, block], back, 1),
        pltpu.roll(units[cell, later], back, 1),
    )
    row = lax.broadcasted_iota(jnp.int32, (8, LANES), 0)
    for axis in range(3):
        chunk = chunk + jnp.where(row == axis, jnp.float32(moves[axis]), 0.0)
    if force:
        root = cbrt(chunk[ROW_Q : ROW_Q + 1])
        own_root = cbrt(chunk[ROW_Q : ROW_Q + 1] / chunk[4:5])
        inv_h = chunk[3:4]
        chunk = jnp.concatenate(
            [chunk[0:3], root * inv_h, chunk[4:5], own_root, root, own_root * inv_h], axis=0
        )
    return jnp.where(lane < count, chunk, FAR)


def pack(shift, units, meta, chunks, extra_of, extra_first, force):
    most = jnp.int32(0)
    for gx, gy, gz in itertools.product(range(4), repeat=3):
        g = gx * 16 + gy * 4 + gz
        cell, octant, moves = octant_place(gx, gy, gz, shift)
        first, count = whole(meta[cell, octant]), whole(meta[cell, octant + 8])
        most = jnp.maximum(most, count)
        chunks[g] = taken(units, cell, first, count, moves, force)

    def all_extra():
        def octants(g, used):
            cell, octant, moves = octant_place(g // 16, g // 4 % 4, g % 4, shift)
            first, count = whole(meta[cell, octant]), whole(meta[cell, octant + 8])
            more = jnp.maximum((count + LANES - 1) // LANES - 1, 0)
            extra_first[g] = used

            def one(k, _):
                done = (k + 1) * LANES
                extra_of[used + k] = g
                chunks[64 + used + k] = taken(
                    units,
                    cell,
                    first + done,
                    count - done,
                    [m.astype(jnp.float32) for m in moves],
                    force,
                )
                return 0

            lax.fori_loop(0, more, one, 0)
            return used + more

        return lax.fori_loop(0, 64, octants, jnp.int32(0))

    return lax.cond(most > LANES, all_extra, lambda: jnp.int32(0))


def near(g, other):
    close = lambda a, b: (a - b <= 1) & (b - a <= 1)
    return (
        close(g // 16, other // 16)
        & close(g // 4 % 4, other // 4 % 4)
        & close(g % 4, other % 4)
    )


def sweep(shift, meta, chunks, columns, extra_of, extra_first, extra_near, used, fields, terms, finish):
    def octant_step(index, _):
        gx, gy, gz = 1 + index // 4, 1 + index // 2 % 2, 1 + index % 2
        g = gx * 16 + gy * 4 + gz
        cell, octant, _ = octant_place(gx, gy, gz, shift)
        first, live = whole(meta[cell, octant]), whole(meta[cell, octant + 16])

        def note(k, kept):
            extra_near[kept] = 64 + k
            return kept + jnp.where(near(g, extra_of[k]), 1, 0)

        kept = lax.fori_loop(0, used, note, jnp.int32(0))

        def chunk_step(part, _):
            at = jnp.where(part == 0, g, 64 + extra_first[g] + part - 1)
            columns[0:LANES, 0:8] = chunks[at].T
            here = jnp.minimum(live - part * LANES, LANES)

            def rows_step(k, _):
                rows = pl.ds(pl.multiple_of(k * IROWS, IROWS), IROWS)
                own = [
                    jnp.broadcast_to(columns[rows, f : f + 1], (IROWS, LANES)) for f in fields
                ]
                acc = None
                for offset in OFFSETS:
                    acc = terms(own, chunks, g + offset, acc)
                acc = lax.fori_loop(
                    0, kept, lambda n, acc: terms(own, chunks, extra_near[n], acc), acc
                )
                lane = lax.broadcasted_iota(jnp.int32, (IROWS, LANES), 1)
                out = jnp.zeros((IROWS, LANES), jnp.float32)
                for n, a in enumerate(acc):
                    out = jnp.where(lane == n, jnp.sum(a, axis=1, keepdims=True), out)
                columns[pl.ds(pl.multiple_of(LANES + k * IROWS, IROWS), IROWS), :] = out
                return 0

            lax.fori_loop(0, (here + IROWS - 1) // IROWS, rows_step, 0)
            result = columns[LANES : 2 * LANES, :].T[0:8]
            finish(cell, first + part * LANES, here, result, chunks[at])
            return 0

        lax.fori_loop(0, (live + LANES - 1) // LANES, chunk_step, 0)
        return 0

    lax.fori_loop(0, 8, octant_step, 0)


def put(ref, first, count, rows):
    block = jnp.minimum(first // LANES, BLOCKS - 1)
    later = jnp.minimum(block + 1, BLOCKS - 1)
    turn = first % LANES
    turned = pltpu.roll(rows, turn, 1)
    lane = lax.broadcasted_iota(jnp.int32, rows.shape, 1)
    ref[block] = jnp.where((lane >= turn) & (lane < turn + count), turned, ref[block])
    ref[later] = jnp.where(lane < turn + count - LANES, turned, ref[later])


def distance(own, j):
    dx, dy, dz = own[0] - j[0:1], own[1] - j[1:2], own[2] - j[2:3]
    d2 = dx * dx + dy * dy + dz * dz
    return dx, dy, dz, d2 * lax.rsqrt(jnp.maximum(d2, 1e-30))


def density_terms(own, chunks, at, acc):
    j = chunks[at]
    _, _, _, dist = distance(own, j)
    rest = jnp.maximum(1.0 - dist * own[3], 0.0)
    rest2 = rest * rest
    term = (rest2 * rest2) * (1.25 - rest) * j[4:5]
    return (term,) if acc is None else (acc[0] + term,)


def force_terms(own, chunks, at, acc):
    j = chunks[at]
    dx, dy, dz, dist = distance(own, j)
    rest_own = jnp.maximum(own[3] - dist * own[4], 0.0)
    rest_far = jnp.maximum(j[6:7] - dist * j[3:4], 0.0)
    coef = j[4:5] * (rest_own * rest_own * rest_own) + rest_far * rest_far * rest_far
    terms = (coef * dx, coef * dy, coef * dz)
    return terms if acc is None else tuple(a + t for a, t in zip(acc, terms))


def read_counts(units, meta, sem, cells):
    copies = [
        pltpu.make_async_copy(units.at[c, 0, ROW_META], meta.at[c], sem.at[c]) for c in range(cells)
    ]
    for copy in copies:
        copy.start()
    for copy in copies:
        copy.wait()


def density_kernel(units, q_ref, meta, chunks, columns, extra_of, extra_first, extra_near, sem):
    read_counts(units, meta, sem, 8)
    for c in range(8):
        q_ref[c] = units[c, :, ROW_Q : ROW_Q + 1, :]
    used = pack(0, units, meta, chunks, extra_of, extra_first, False)

    def finish(cell, first, count, result, chunk):
        ih = chunk[3:4]
        rho = (4.0 * KW) * result[0:1] * (ih * ih * ih)
        q = chunk[5:6] * inv_cbrt(jnp.maximum(rho, 1e-30))
        put(q_ref.at[cell], first, count, q)

    sweep(
        0, meta, chunks, columns, extra_of, extra_first, extra_near, used, (0, 1, 2, 3),
        density_terms, finish,
    )


def force_kernel(
    units, rank_ref, old_ref, act_ref, dens_ref, acc_ref,
    meta, chunks, columns, extra_of, extra_first, extra_near, found, sem,
):
    read_counts(units, meta, sem, 27)
    used = pack(1, units, meta, chunks, extra_of, extra_first, True)
    found[...] = jnp.zeros_like(found)

    def finish(cell, first, count, result, chunk):
        put(found, first, count, result)

    sweep(
        1, meta, chunks, columns, extra_of, extra_first, extra_near, used, (0, 1, 2, 5, 7),
        force_terms, finish,
    )
    row = lax.broadcasted_iota(jnp.int32, (8, LANES), 0)
    parts = []
    for k in range(BLOCKS):
        ratio = units[13, k, 5:6, :] / units[13, k, ROW_Q : ROW_Q + 1, :]
        parts.append(jnp.where(row == 3, ratio * ratio * ratio, found[k] * KG))
    back = jnp.dot(
        split3(jnp.concatenate(parts, axis=1)), one_hot_of(rank_ref[...]),
        preferred_element_type=jnp.float32,
    )
    back = join3(back)
    live = act_ref[...] == 1
    acc_ref[...] = jnp.where(live, back[0:3], 0.0)
    dens_ref[...] = jnp.where(live, back[3:4], old_ref[...])


def vmem(n):
    return [pl.BlockSpec(memory_space=pltpu.VMEM)] * n


PARAMS = pltpu.CompilerParams(vmem_limit_bytes=24 * 1024 * 1024)


def scratch(cells, extra):
    return [
        pltpu.SMEM((cells, LANES), jnp.float32),
        pltpu.VMEM((64 + extra, 8, LANES), jnp.float32),
        pltpu.VMEM((2 * LANES, LANES), jnp.float32),
        pltpu.SMEM((extra,), jnp.int32),
        pltpu.SMEM((64,), jnp.int32),
        pltpu.SMEM((extra + 1,), jnp.int32),
    ]


def shape(*dims):
    return jax.ShapeDtypeStruct(dims, jnp.float32)


def from_next(block, axis):
    count = lax.axis_size(axis)
    return lax.ppermute(block, axis, [(i, (i - 1) % count) for i in range(count)])


def from_last(block, axis):
    count = lax.axis_size(axis)
    return lax.ppermute(block, axis, [(i, (i + 1) % count) for i in range(count)])


def body(positions, smoothing, masses, entropy, old_density, active):
    row = lambda a: a.reshape(1, COUNT)
    unit, rank = pl.pallas_call(
        sort_kernel,
        out_shape=(shape(BLOCKS, 8, LANES), jax.ShapeDtypeStruct((1, COUNT), jnp.int32)),
        in_specs=vmem(6),
        out_specs=tuple(vmem(2)),
        compiler_params=PARAMS,
        name="sort_octants",
    )(
        positions.reshape(3, COUNT), row(smoothing), row(masses), row(entropy), row(old_density),
        row(active),
    )
    units = unit[None, None, None]
    for dim, axis in ((0, "gx"), (1, "gy"), (2, "gz")):
        units = jnp.concatenate([units, from_next(units, axis)], axis=dim)
    q = pl.pallas_call(
        density_kernel,
        out_shape=shape(8, BLOCKS, 1, LANES),
        in_specs=vmem(1),
        out_specs=vmem(1)[0],
        scratch_shapes=scratch(8, 40) + [pltpu.SemaphoreType.DMA((8,))],
        compiler_params=PARAMS,
        name="density",
    )(units.reshape(8, BLOCKS, 8, LANES))
    q = q.reshape(2, 2, 2, BLOCKS, 1, LANES)
    units = jnp.concatenate([units[..., :ROW_Q, :], q, units[..., ROW_Q + 1 :, :]], axis=-2)
    for dim, axis in ((0, "gx"), (1, "gy"), (2, "gz")):
        low = lax.slice_in_dim(units, 0, 1, axis=dim)
        high = lax.slice_in_dim(units, 1, 2, axis=dim)
        high_q = high[..., ROW_Q, :]
        sent = jnp.concatenate([low.reshape(-1, LANES), high_q.reshape(-1, LANES)], axis=0)
        got = from_last(sent, axis)
        size = low.size // LANES
        far = got[:size].reshape(low.shape)
        far_q = got[size:].reshape(high_q.shape)
        low_q = jnp.where(low[..., dim, :] < 0.5, far_q, low[..., ROW_Q, :])
        low = jnp.concatenate(
            [low[..., :ROW_Q, :], low_q[..., None, :], low[..., ROW_Q + 1 :, :]], axis=-2
        )
        units = jnp.concatenate([far, low, high], axis=dim)
    dens, accel = pl.pallas_call(
        force_kernel,
        out_shape=(shape(1, COUNT), shape(3, COUNT)),
        in_specs=vmem(4),
        out_specs=tuple(vmem(2)),
        scratch_shapes=scratch(27, 136)
        + [pltpu.VMEM((BLOCKS, 8, LANES), jnp.float32), pltpu.SemaphoreType.DMA((27,))],
        compiler_params=PARAMS,
        name="force",
    )(units.reshape(27, BLOCKS, 8, LANES), rank, row(old_density), row(active))
    return dens.reshape(1, 1, 1, COUNT), accel.reshape(1, 1, 1, 3, COUNT)


def solution(mesh):
    cells = P("gx", "gy", "gz", None)
    vectors = P("gx", "gy", "gz", None, None)
    return jax.shard_map(
        body,
        mesh=mesh,
        in_specs=(vectors, cells, cells, cells, cells, cells),
        out_specs=(cells, vectors),
        check_vma=False,
    )
```

```python
import itertools
import math

import jax
import jax.numpy as jnp
from jax import lax
from jax.experimental import pallas as pl
from jax.experimental.pallas import tpu as pltpu
from jax.sharding import PartitionSpec as P

KW = 21.0 / (2.0 * math.pi)
KG = 210.0 / math.pi
LANES = 128
COUNT = 768
BLOCKS = COUNT // LANES
FAR = 1.0e4
IROWS = 16
GROUPS = IROWS // 8
RUN = 3
RUNS = 32
ROW_C = 6
ROW_META = 7


def cbrt(x):
    return jnp.exp(jnp.log(x) * (1.0 / 3.0))


def inv_cbrt(x):
    return jnp.exp(jnp.log(x) * (-1.0 / 3.0))


def split3(rows):
    hi = rows.astype(jnp.bfloat16).astype(jnp.float32)
    rest = rows - hi
    mid = rest.astype(jnp.bfloat16).astype(jnp.float32)
    low = rest - mid
    return jnp.concatenate([hi, mid, low, jnp.zeros_like(hi)], axis=0).astype(jnp.bfloat16)


def join3(parts):
    return parts[0:8] + parts[8:16] + parts[16:24]


def one_hot_of(rank):
    place = lax.broadcasted_iota(jnp.int32, (COUNT, COUNT), 0)
    return (place == rank).astype(jnp.float32).astype(jnp.bfloat16)


def sort_kernel(pos_ref, h_ref, m_ref, a_ref, old_ref, act_ref, unit_ref, rank_ref):
    x, y, z = pos_ref[0:1], pos_ref[1:2], pos_ref[2:3]
    ih = 1.0 / h_ref[...]
    ih2 = ih * ih
    mass = m_ref[...]
    b = mass * a_ref[...] * (ih2 * ih2 * ih)
    c = cbrt(b * inv_cbrt(old_ref[...]))
    one, zero = jnp.int32(1), jnp.int32(0)
    key = (
        jnp.where(x >= 0.5, 8 * one, zero)
        + jnp.where(y >= 0.5, 4 * one, zero)
        + jnp.where(z >= 0.5, 2 * one, zero)
        + jnp.where(act_ref[...] == 1, zero, one)
    )
    kind = lax.broadcasted_iota(jnp.int32, (16, COUNT), 0)
    hot = (kind == key).astype(jnp.float32)
    blocks = jnp.concatenate([hot[:, k * LANES : (k + 1) * LANES] for k in range(BLOCKS)], axis=0)
    before = lax.broadcasted_iota(jnp.int32, (LANES, LANES), 0)
    after = lax.broadcasted_iota(jnp.int32, (LANES, LANES), 1)
    upper = (before < after).astype(jnp.float32).astype(jnp.bfloat16)
    prefix = jnp.dot(blocks.astype(jnp.bfloat16), upper, preferred_element_type=jnp.float32)
    sums = [jnp.sum(hot[:, k * LANES : (k + 1) * LANES], axis=1, keepdims=True) for k in range(BLOCKS)]
    running = jnp.zeros((16, 1), jnp.float32)
    carried = []
    for k in range(BLOCKS):
        carried.append(prefix[16 * k : 16 * (k + 1)] + running)
        running = running + sums[k]
    total = jnp.broadcast_to(running, (16, LANES))
    start = jnp.zeros((16, LANES), jnp.float32)
    row = lax.broadcasted_iota(jnp.int32, (16, LANES), 0)
    for k in range(15):
        start = start + jnp.where(row > k, total[k : k + 1], 0.0)
    rank = jnp.concatenate(
        [
            jnp.sum(
                hot[:, k * LANES : (k + 1) * LANES] * (carried[k] + start), axis=0, keepdims=True
            )
            for k in range(BLOCKS)
        ],
        axis=1,
    ).astype(jnp.int32)
    rank_ref[...] = rank
    rows = jnp.concatenate([x, y, z, ih, mass, b, c, jnp.zeros_like(c)], axis=0)
    moved = lax.dot_general(
        split3(rows), one_hot_of(rank), (((1,), (1,)), ((), ())), preferred_element_type=jnp.float32
    )
    moved = join3(moved)
    lane = lax.broadcasted_iota(jnp.int32, (16, LANES), 1)
    even = (row & 1) == 0
    octant = row >> 1
    counts = (
        jnp.where((lane == octant) & even, start, 0.0)
        + jnp.where(lane == octant + 8, total, 0.0)
        + jnp.where((lane == octant + 16) & even, total, 0.0)
    )
    counts = jnp.sum(counts, axis=0, keepdims=True)
    which = lax.broadcasted_iota(jnp.int32, (8, LANES), 0)
    for k in range(BLOCKS):
        unit_ref[k] = jnp.where(which == ROW_META, counts, moved[:, k * LANES : (k + 1) * LANES])


def whole(value):
    return value.astype(jnp.int32)


def real(value):
    return jnp.float32(value) if isinstance(value, int) else value.astype(jnp.float32)


def lanes_of(shape=(8, LANES)):
    return lax.broadcasted_iota(jnp.int32, shape, len(shape) - 1)


def windows(units, cell, first, number):
    block, turn = first >> 7, first & (LANES - 1)
    back = (LANES - turn) & (LANES - 1)
    turned = [
        pltpu.roll(units[cell, jnp.clip(block + k, 0, BLOCKS - 1)], back, 1)
        for k in range(number + 1)
    ]
    keep = lanes_of() < LANES - turn
    return [jnp.where(keep, turned[k], turned[k + 1]) for k in range(number)]


def moved_by(chunk, moves):
    row = lax.broadcasted_iota(jnp.int32, (8, LANES), 0)
    step = jnp.float32(0.0)
    for axis in range(3):
        step = jnp.where(row == axis, jnp.float32(moves[axis]), step)
    return chunk + step


def cell_of(cx, cy, cz, shift):
    side = 2 + shift
    return (cx * side + cy) * side + cz


def run_parts(gx, gy, side, shift, meta):
    ex, ey = gx + shift, gy + shift
    cx, cy = ex // 2, ey // 2
    octant = (ex % 2) * 4 + (ey % 2) * 2
    last = jnp.int32(side == shift) if isinstance(side, int) else (side == shift).astype(jnp.int32)
    parts = []
    for which in range(2):
        cz = which + (side if shift else 0)
        half = last if which else 1 - last
        cell = cell_of(cx, cy, cz, shift)
        first_octant = octant + (0 if which else half)
        first = whole(meta[cell, first_octant])
        count = whole(meta[cell, first_octant + 8])
        count = count + jnp.where(half == 1, 0, whole(meta[cell, octant + 9]))
        parts.append((cell, first, count, (cx, cy, cz)))
    return parts


def run_chunks(units, parts, begin, number, force):
    (cell_a, first_a, count_a, moves_a), (cell_b, first_b, count_b, moves_b) = parts
    a = windows(units, cell_a, first_a + begin, number)
    b = windows(units, cell_b, first_b + begin - count_a, number)
    out = []
    for k in range(number):
        lane = lanes_of() + (begin + k * LANES)
        chunk = jnp.where(lane < count_a, moved_by(a[k], moves_a), moved_by(b[k], moves_b))
        chunk = jnp.where(lane < count_a + count_b, chunk, FAR)
        x, y, z, ih, m, c = (chunk[f : f + 1] for f in (0, 1, 2, 3, 4, ROW_C))
        out.append((x, y, z, m, c, c * ih) if force else (x, y, z, m))
    return out


def store_chunk(chunks, at, rows):
    for f, values in enumerate(rows):
        chunks[at, f] = jnp.broadcast_to(values, (8, LANES))


def pack(shift, units, meta, chunks, extra_first, force):
    longest = jnp.int32(0)
    for gx, gy, side in itertools.product(range(4), range(4), range(2)):
        run = (gx * 4 + gy) * 2 + side
        parts = run_parts(gx, gy, side, shift, meta)
        longest = jnp.maximum(longest, parts[0][2] + parts[1][2])
        for k, rows in enumerate(run_chunks(units, parts, jnp.int32(0), RUN, force)):
            store_chunk(chunks, run * RUN + k, rows)

    @pl.when(longest > RUN * LANES)
    def _():
        def long_run(run, used):
            parts = run_parts(run // 8, run // 2 % 4, run % 2, shift, meta)
            parts = [(c, f, n, [real(v) for v in mv]) for c, f, n, mv in parts]
            more = jnp.maximum((parts[0][2] + parts[1][2] + LANES - 1) // LANES - RUN, 0)
            extra_first[run] = used

            def one(k, _):
                rows = run_chunks(units, parts, (k + RUN) * LANES, 1, force)[0]
                store_chunk(chunks, RUNS * RUN + used + k, rows)
                return 0

            lax.fori_loop(0, more, one, 0)
            return used + more

        extra_first[RUNS] = lax.fori_loop(0, RUNS, long_run, jnp.int32(0))

    return longest


def own_octant(index, shift, meta):
    ix, iy, iz = index // 4, index // 2 % 2, index % 2
    if shift:
        moves, octant = (1, 1, 1), index
    else:
        moves, octant = (ix, iy, iz), 7 - index
    cell = cell_of(*moves, shift)
    run = ((1 + ix) * 4 + 1 + iy) * 2 + iz
    return cell, octant, moves, run


def own_chunk(units, cell, first, live, moves, force):
    chunk = moved_by(windows(units, cell, first, 1)[0], moves)
    if force:
        c = chunk[ROW_C : ROW_C + 1] / cbrt(chunk[4:5])
        chunk = jnp.concatenate([chunk[0:3], c, c * chunk[3:4], chunk[5:8]], axis=0)
    return jnp.where(lanes_of() < live, chunk, FAR)


def store_columns(columns, slot, chunk, fields):
    turned = chunk.T
    for f in range(fields):
        columns[slot, f] = jnp.broadcast_to(turned[:, f : f + 1], (LANES, LANES))


def sweep_rows(slot, run, live, kept, chunks, columns, sums, extra_near, fields, terms):
    def rows_step(k, _):
        at = pl.multiple_of(k * IROWS, IROWS)
        own = [
            [columns[slot, f, pl.ds(at + 8 * g, 8), :] for f in range(fields)]
            for g in range(GROUPS)
        ]
        acc = [None] * GROUPS
        for dx, dy, n in itertools.product((-1, 0, 1), (-1, 0, 1), range(RUN)):
            acc = terms(own, chunks, (run + dx * 8 + dy * 2) * RUN + n, acc)
        acc = lax.fori_loop(
            0, kept, lambda n, acc: terms(own, chunks, extra_near[n], acc), acc
        )
        for g in range(GROUPS):
            for n, a in enumerate(acc[g]):
                sums[slot, n, pl.ds(at + 8 * g, 8), :] = a
        return 0

    lax.fori_loop(0, (live + IROWS - 1) // IROWS, rows_step, 0)


def gathered(sums, slot, number):
    out = []
    diagonal = lanes_of() - lax.broadcasted_iota(jnp.int32, (8, LANES), 0)
    for n in range(number):
        total = jnp.zeros((8, LANES), jnp.float32)
        for k in range(LANES // 8):
            part = jnp.sum(sums[slot, n, 8 * k : 8 * k + 8, :], axis=1, keepdims=True)
            total = jnp.where(diagonal == 8 * k, part, total)
        out.append(jnp.sum(total, axis=0, keepdims=True))
    return out


def note_extra(run, extra_first, extra_near):
    kept = jnp.int32(0)
    for dx, dy in itertools.product((-1, 0, 1), repeat=2):
        beside = run + dx * 8 + dy * 2
        first = extra_first[beside]

        def note(k, _, first=first, kept=kept):
            extra_near[kept + k] = RUNS * RUN + first + k
            return 0

        number = extra_first[beside + 1] - first
        lax.fori_loop(0, number, note, 0)
        kept = kept + number
    return kept


def sweep(shift, units, meta, chunks, columns, sums, extra_first, extra_near, force, terms, finish):
    fields, number = (5, 3) if force else (4, 1)
    longest = pack(shift, units, meta, chunks, extra_first, force)
    owns = []
    most = jnp.int32(0)
    for index in range(8):
        cell, octant, moves, _ = own_octant(index, shift, meta)
        first, live = whole(meta[cell, octant]), whole(meta[cell, octant + 16])
        most = jnp.maximum(most, live)
        chunk = own_chunk(units, cell, first, live, moves, force)
        store_columns(columns, index, chunk, fields)
        owns.append((cell, first, live, chunk))

    def octant_step(index, _):
        cell, octant, _, run = own_octant(index, shift, meta)
        live = jnp.minimum(whole(meta[cell, octant + 16]), LANES)
        kept = lax.cond(
            longest > RUN * LANES,
            lambda: note_extra(run, extra_first, extra_near),
            lambda: jnp.int32(0),
        )
        sweep_rows(index, run, live, kept, chunks, columns, sums, extra_near, fields, terms)
        return 0

    lax.fori_loop(0, 8, octant_step, 0)
    for index, (cell, first, live, chunk) in enumerate(owns):
        finish(cell, first, jnp.minimum(live, LANES), gathered(sums, index, number), chunk)

    @pl.when(most > LANES)
    def _():
        def octant_rest(index, _):
            cell, octant, moves, run = own_octant(index, shift, meta)
            moves = [real(v) for v in moves]
            first, live = whole(meta[cell, octant]), whole(meta[cell, octant + 16])
            kept = lax.cond(
                longest > RUN * LANES,
                lambda: note_extra(run, extra_first, extra_near),
                lambda: jnp.int32(0),
            )

            def part_step(part, _):
                done = part * LANES
                chunk = own_chunk(units, cell, first + done, live - done, moves, force)
                store_columns(columns, 0, chunk, fields)
                here = jnp.minimum(live - done, LANES)
                sweep_rows(0, run, here, kept, chunks, columns, sums, extra_near, fields, terms)
                finish(cell, first + done, here, gathered(sums, 0, number), chunk)
                return 0

            lax.fori_loop(1, (live + LANES - 1) // LANES, part_step, 0)
            return 0

        lax.fori_loop(0, 8, octant_rest, 0)


def put(ref, first, count, rows):
    block = jnp.minimum(first // LANES, BLOCKS - 1)
    later = jnp.minimum(block + 1, BLOCKS - 1)
    turn = first % LANES
    turned = pltpu.roll(rows, turn, 1)
    lane = lanes_of(rows.shape)
    ref[block] = jnp.where((lane >= turn) & (lane < turn + count), turned, ref[block])
    ref[later] = jnp.where(lane < turn + count - LANES, turned, ref[later])


def distance(own, x, y, z):
    dx, dy, dz = own[0] - x, own[1] - y, own[2] - z
    d2 = dx * dx + dy * dy + dz * dz
    return dx, dy, dz, d2 * lax.rsqrt(jnp.maximum(d2, 1e-30))


def added(acc, terms):
    return terms if acc is None else tuple(a + t for a, t in zip(acc, terms))


def density_terms(own, chunks, at, acc):
    x, y, z, m = (chunks[at, f] for f in range(4))
    out = []
    for g in range(GROUPS):
        dist = distance(own[g], x, y, z)[3]
        rest = jnp.maximum(1.0 - dist * own[g][3], 0.0)
        rest2 = rest * rest
        out.append(added(acc[g], ((rest2 * rest2) * (1.25 - rest) * m,)))
    return out


def force_terms(own, chunks, at, acc):
    x, y, z, m, c, k = (chunks[at, f] for f in range(6))
    out = []
    for g in range(GROUPS):
        dx, dy, dz, dist = distance(own[g], x, y, z)
        rest_own = jnp.maximum(own[g][3] - dist * own[g][4], 0.0)
        rest_far = jnp.maximum(c - dist * k, 0.0)
        coef = m * (rest_own * rest_own * rest_own) + rest_far * rest_far * rest_far
        out.append(added(acc[g], (coef * dx, coef * dy, coef * dz)))
    return out


def read_counts(units, meta, sem):
    copy = pltpu.make_async_copy(units.at[:, 0, ROW_META], meta, sem)
    copy.start()
    copy.wait()


def density_kernel(units, c_ref, meta, chunks, columns, sums, extra_first, extra_near, sem):
    read_counts(units, meta, sem)
    for cell in range(8):
        c_ref[cell] = units[cell, :, ROW_C : ROW_C + 1, :]

    def finish(cell, first, count, result, chunk):
        ih = chunk[3:4]
        rho = (4.0 * KW) * result[0] * (ih * ih * ih)
        c = cbrt(chunk[5:6] * inv_cbrt(jnp.maximum(rho, 1e-30)))
        put(c_ref.at[cell], first, count, c)

    sweep(
        0, units, meta, chunks, columns, sums, extra_first, extra_near, False, density_terms, finish
    )


def force_kernel(
    units, rank_ref, old_ref, act_ref, dens_ref, acc_ref,
    meta, chunks, columns, sums, extra_first, extra_near, sem, found,
):
    read_counts(units, meta, sem)
    found[...] = jnp.zeros_like(found)

    def finish(cell, first, count, result, chunk):
        put(found, first, count, jnp.concatenate(result + [result[0]] * 5, axis=0))

    sweep(
        1, units, meta, chunks, columns, sums, extra_first, extra_near, True, force_terms, finish
    )
    row = lax.broadcasted_iota(jnp.int32, (8, LANES), 0)
    parts = []
    for k in range(BLOCKS):
        c = units[13, k, ROW_C : ROW_C + 1, :]
        ratio = units[13, k, 5:6, :] / (c * c * c)
        parts.append(jnp.where(row == 3, ratio * ratio * ratio, found[k] * KG))
    back = jnp.dot(
        split3(jnp.concatenate(parts, axis=1)), one_hot_of(rank_ref[...]),
        preferred_element_type=jnp.float32,
    )
    back = join3(back)
    live = act_ref[...] == 1
    acc_ref[...] = jnp.where(live, back[0:3], 0.0)
    dens_ref[...] = jnp.where(live, back[3:4], old_ref[...])


def run_density(units):
    return pl.pallas_call(
        density_kernel,
        out_shape=shape(8, BLOCKS, 1, LANES),
        in_specs=vmem(1),
        out_specs=vmem(1)[0],
        scratch_shapes=scratch(8, 96, 4, 1),
        compiler_params=PARAMS,
        name="density",
    )(units)


def run_force(units, rank, old, act):
    return pl.pallas_call(
        force_kernel,
        out_shape=(shape(1, COUNT), shape(3, COUNT)),
        in_specs=vmem(4),
        out_specs=tuple(vmem(2)),
        scratch_shapes=scratch(27, 324, 6, 3) + [pltpu.VMEM((BLOCKS, 8, LANES), jnp.float32)],
        compiler_params=PARAMS,
        name="force",
    )(units, rank, old, act)


def vmem(n):
    return [pl.BlockSpec(memory_space=pltpu.VMEM)] * n


PARAMS = pltpu.CompilerParams(vmem_limit_bytes=40 * 1024 * 1024)


def scratch(cells, extra, rows, number):
    return [
        pltpu.SMEM((cells, LANES), jnp.float32),
        pltpu.VMEM((RUNS * RUN + extra, rows, 8, LANES), jnp.float32),
        pltpu.VMEM((8, 5, LANES, LANES), jnp.float32),
        pltpu.VMEM((8, number, LANES, LANES), jnp.float32),
        pltpu.SMEM((RUNS + 1,), jnp.int32),
        pltpu.SMEM((extra + 1,), jnp.int32),
        pltpu.SemaphoreType.DMA,
    ]


def shape(*dims):
    return jax.ShapeDtypeStruct(dims, jnp.float32)


def from_next(block, axis):
    count = lax.axis_size(axis)
    return lax.ppermute(block, axis, [(i, (i - 1) % count) for i in range(count)])


def from_last(block, axis):
    count = lax.axis_size(axis)
    return lax.ppermute(block, axis, [(i, (i + 1) % count) for i in range(count)])


def body(positions, smoothing, masses, entropy, old_density, active):
    row = lambda a: a.reshape(1, COUNT)
    unit, rank = pl.pallas_call(
        sort_kernel,
        out_shape=(shape(BLOCKS, 8, LANES), jax.ShapeDtypeStruct((1, COUNT), jnp.int32)),
        in_specs=vmem(6),
        out_specs=tuple(vmem(2)),
        compiler_params=PARAMS,
        name="sort_octants",
    )(
        positions.reshape(3, COUNT), row(smoothing), row(masses), row(entropy), row(old_density),
        row(active),
    )
    units = unit[None, None, None]
    for dim, axis in ((0, "gx"), (1, "gy"), (2, "gz")):
        units = jnp.concatenate([units, from_next(units, axis)], axis=dim)
    c = run_density(units.reshape(8, BLOCKS, 8, LANES)).reshape(2, 2, 2, BLOCKS, 1, LANES)
    units = jnp.concatenate([units[..., :ROW_C, :], c, units[..., ROW_C + 1 :, :]], axis=-2)
    for dim, axis in ((0, "gx"), (1, "gy"), (2, "gz")):
        low = lax.slice_in_dim(units, 0, 1, axis=dim)
        high = lax.slice_in_dim(units, 1, 2, axis=dim)
        high_c = high[..., ROW_C, :]
        sent = jnp.concatenate([low.reshape(-1, LANES), high_c.reshape(-1, LANES)], axis=0)
        got = from_last(sent, axis)
        size = low.size // LANES
        far = got[:size].reshape(low.shape)
        far_c = got[size:].reshape(high_c.shape)
        low_c = jnp.where(low[..., dim, :] < 0.5, far_c, low[..., ROW_C, :])
        low = jnp.concatenate(
            [low[..., :ROW_C, :], low_c[..., None, :], low[..., ROW_C + 1 :, :]], axis=-2
        )
        units = jnp.concatenate([far, low, high], axis=dim)
    dens, accel = run_force(
        units.reshape(27, BLOCKS, 8, LANES), rank, row(old_density), row(active)
    )
    return dens.reshape(1, 1, 1, COUNT), accel.reshape(1, 1, 1, 3, COUNT)


def solution(mesh):
    cells = P("gx", "gy", "gz", None)
    vectors = P("gx", "gy", "gz", None, None)
    return jax.shard_map(
        body,
        mesh=mesh,
        in_specs=(vectors, cells, cells, cells, cells, cells),
        out_specs=(cells, vectors),
        check_vma=False,
    )
```

```python
import itertools
import math

import jax
import jax.numpy as jnp
from jax import lax
from jax.experimental import pallas as pl
from jax.experimental.pallas import tpu as pltpu
from jax.sharding import PartitionSpec as P

KW = 21.0 / (2.0 * math.pi)
KG = 210.0 / math.pi
LANES = 128
COUNT = 768
BLOCKS = COUNT // LANES
FAR = 1.0e4
IROWS = 16
GROUPS = IROWS // 8
RUN = 3
RUNS = 32
ROW_C = 6
ROW_META = 7


def cbrt(x):
    return jnp.exp(jnp.log(x) * (1.0 / 3.0))


def inv_cbrt(x):
    return jnp.exp(jnp.log(x) * (-1.0 / 3.0))


def parts3(rows):
    hi = rows.astype(jnp.bfloat16).astype(jnp.float32)
    rest = rows - hi
    mid = rest.astype(jnp.bfloat16).astype(jnp.float32)
    return jnp.concatenate([hi, mid, rest - mid, jnp.zeros_like(hi)], axis=0)


def split3(rows):
    return parts3(rows).astype(jnp.bfloat16)


def join3(parts):
    return parts[0:8] + parts[8:16] + parts[16:24]


def one_hot_of(rank):
    place = lax.broadcasted_iota(jnp.int32, (COUNT, COUNT), 0)
    return (place == rank).astype(jnp.float32).astype(jnp.bfloat16)


def sort_kernel(pos_ref, h_ref, m_ref, a_ref, old_ref, act_ref, unit_ref, hot_ref):
    x, y, z = pos_ref[0], pos_ref[1], pos_ref[2]
    ih = 1.0 / h_ref[...]
    ih2 = ih * ih
    mass = m_ref[...]
    b = mass * a_ref[...] * (ih2 * ih2 * ih)
    c = cbrt(b * inv_cbrt(old_ref[...]))
    one, zero = jnp.int32(1), jnp.int32(0)
    key = (
        jnp.where(x >= 0.5, 8 * one, zero)
        + jnp.where(y >= 0.5, 4 * one, zero)
        + jnp.where(z >= 0.5, 2 * one, zero)
        + jnp.where(act_ref[...] == 1, zero, one)
    )
    kind = lax.broadcasted_iota(jnp.int32, (16, COUNT), 0)
    hot = (kind == key).astype(jnp.float32)
    blocks = jnp.concatenate([hot[:, k * LANES : (k + 1) * LANES] for k in range(BLOCKS)], axis=0)
    before = lax.broadcasted_iota(jnp.int32, (LANES, LANES), 0)
    after = lax.broadcasted_iota(jnp.int32, (LANES, LANES), 1)
    upper = (before < after).astype(jnp.float32).astype(jnp.bfloat16)
    prefix = jnp.dot(blocks.astype(jnp.bfloat16), upper, preferred_element_type=jnp.float32)
    sums = [jnp.sum(hot[:, k * LANES : (k + 1) * LANES], axis=1, keepdims=True) for k in range(BLOCKS)]
    running = jnp.zeros((16, 1), jnp.float32)
    carried = []
    for k in range(BLOCKS):
        carried.append(prefix[16 * k : 16 * (k + 1)] + running)
        running = running + sums[k]
    total = jnp.broadcast_to(running, (16, LANES))
    start = jnp.zeros((16, LANES), jnp.float32)
    row = lax.broadcasted_iota(jnp.int32, (16, LANES), 0)
    for k in range(15):
        start = start + jnp.where(row > k, total[k : k + 1], 0.0)
    rank = jnp.concatenate(
        [
            jnp.sum(
                hot[:, k * LANES : (k + 1) * LANES] * (carried[k] + start), axis=0, keepdims=True
            )
            for k in range(BLOCKS)
        ],
        axis=1,
    ).astype(jnp.int32)
    moves = one_hot_of(rank)
    hot_ref[...] = moves
    rows = jnp.concatenate([x, y, z, ih, mass, b, c, jnp.zeros_like(c)], axis=0)
    moved = lax.dot_general(
        split3(rows), moves, (((1,), (1,)), ((), ())), preferred_element_type=jnp.float32
    )
    moved = join3(moved)
    lane = lax.broadcasted_iota(jnp.int32, (16, LANES), 1)
    even = (row & 1) == 0
    octant = row >> 1
    counts = (
        jnp.where((lane == octant) & even, start, 0.0)
        + jnp.where(lane == octant + 8, total, 0.0)
        + jnp.where((lane == octant + 16) & even, total, 0.0)
    )
    counts = jnp.sum(counts, axis=0, keepdims=True)
    which = lax.broadcasted_iota(jnp.int32, (8, LANES), 0)
    for k in range(BLOCKS):
        unit_ref[k] = jnp.where(which == ROW_META, counts, moved[:, k * LANES : (k + 1) * LANES])


def real(value):
    return jnp.float32(value) if isinstance(value, int) else value.astype(jnp.float32)


def lanes_of(shape=(8, LANES)):
    return lax.broadcasted_iota(jnp.int32, shape, len(shape) - 1)


def windows(units, cell, first, number):
    block, turn = first >> 7, first & (LANES - 1)
    back = (LANES - turn) & (LANES - 1)
    turned = [
        pltpu.roll(units[cell, jnp.clip(block + k, 0, BLOCKS - 1)], back, 1)
        for k in range(number + 1)
    ]
    keep = lanes_of() < LANES - turn
    return [jnp.where(keep, turned[k], turned[k + 1]) for k in range(number)]


def moved_by(chunk, moves):
    row = lax.broadcasted_iota(jnp.int32, (8, LANES), 0)
    step = jnp.float32(0.0)
    for axis in range(3):
        step = jnp.where(row == axis, jnp.float32(moves[axis]), step)
    return chunk + step


def cell_of(cx, cy, cz, shift):
    side = 2 + shift
    return (cx * side + cy) * side + cz


def run_parts(gx, gy, side, shift, meta):
    ex, ey = gx + shift, gy + shift
    cx, cy = ex // 2, ey // 2
    octant = (ex % 2) * 4 + (ey % 2) * 2
    last = jnp.int32(side == shift) if isinstance(side, int) else (side == shift).astype(jnp.int32)
    parts = []
    for which in range(2):
        cz = which + (side if shift else 0)
        half = last if which else 1 - last
        cell = cell_of(cx, cy, cz, shift)
        first_octant = octant + (0 if which else half)
        first = meta[cell, first_octant]
        count = meta[cell, first_octant + 8]
        count = count + jnp.where(half == 1, 0, meta[cell, octant + 9])
        parts.append((cell, first, count, (cx, cy, cz)))
    return parts


def run_chunks(units, parts, begin, number, force):
    (cell_a, first_a, count_a, moves_a), (cell_b, first_b, count_b, moves_b) = parts
    a = windows(units, cell_a, first_a + begin, number)
    b = windows(units, cell_b, first_b + begin - count_a, number)
    out = []
    for k in range(number):
        lane = lanes_of() + (begin + k * LANES)
        chunk = jnp.where(lane < count_a, moved_by(a[k], moves_a), moved_by(b[k], moves_b))
        chunk = jnp.where(lane < count_a + count_b, chunk, FAR)
        x, y, z, ih, m, c = (chunk[f : f + 1] for f in (0, 1, 2, 3, 4, ROW_C))
        out.append((x, y, z, m, c, c * ih) if force else (x, y, z, m))
    return out


def store_chunk(chunks, at, rows):
    for f, values in enumerate(rows):
        chunks[at, f] = jnp.broadcast_to(values, (8, LANES))


def pack(shift, units, meta, chunks, extra_first, force):
    longest = jnp.int32(0)
    for gx, gy, side in itertools.product(range(4), range(4), range(2)):
        run = (gx * 4 + gy) * 2 + side
        parts = run_parts(gx, gy, side, shift, meta)
        longest = jnp.maximum(longest, parts[0][2] + parts[1][2])
        for k, rows in enumerate(run_chunks(units, parts, jnp.int32(0), RUN, force)):
            store_chunk(chunks, run * RUN + k, rows)

    @pl.when(longest > RUN * LANES)
    def _():
        def long_run(run, used):
            parts = run_parts(run // 8, run // 2 % 4, run % 2, shift, meta)
            parts = [(c, f, n, [real(v) for v in mv]) for c, f, n, mv in parts]
            more = jnp.maximum((parts[0][2] + parts[1][2] + LANES - 1) // LANES - RUN, 0)
            extra_first[run] = used

            def one(k, _):
                rows = run_chunks(units, parts, (k + RUN) * LANES, 1, force)[0]
                store_chunk(chunks, RUNS * RUN + used + k, rows)
                return 0

            lax.fori_loop(0, more, one, 0)
            return used + more

        extra_first[RUNS] = lax.fori_loop(0, RUNS, long_run, jnp.int32(0))

    return longest


def own_octant(index, shift, meta):
    ix, iy, iz = index // 4, index // 2 % 2, index % 2
    if shift:
        moves, octant = (1, 1, 1), index
    else:
        moves, octant = (ix, iy, iz), 7 - index
    cell = cell_of(*moves, shift)
    run = ((1 + ix) * 4 + 1 + iy) * 2 + iz
    return cell, octant, moves, run


def own_chunk(units, cell, first, live, moves, force):
    chunk = moved_by(windows(units, cell, first, 1)[0], moves)
    if force:
        c = chunk[ROW_C : ROW_C + 1] / cbrt(chunk[4:5])
        chunk = jnp.concatenate([chunk[0:3], c, c * chunk[3:4], chunk[5:8]], axis=0)
    return jnp.where(lanes_of() < live, chunk, FAR)


def store_columns(columns, slot, chunk, fields):
    part = lax.broadcasted_iota(jnp.int32, (32, fields * LANES), 0)
    field = lax.broadcasted_iota(jnp.int32, (32, fields * LANES), 1) // LANES
    pick = ((part & 7) == field) & (part < 24)
    values = jnp.dot(
        parts3(chunk).T.astype(jnp.bfloat16), pick.astype(jnp.float32).astype(jnp.bfloat16),
        preferred_element_type=jnp.float32,
    )
    for f in range(fields):
        columns[slot, f] = values[:, f * LANES : (f + 1) * LANES]


def sweep_rows(slot, run, live, kept, chunks, columns, sums, extra_near, fields, terms):
    def rows_step(k, _):
        at = pl.multiple_of(k * IROWS, IROWS)
        own = [
            [columns[slot, f, pl.ds(at + 8 * g, 8), :] for f in range(fields)]
            for g in range(GROUPS)
        ]
        acc = [None] * GROUPS
        for dx, dy, n in itertools.product((-1, 0, 1), (-1, 0, 1), range(RUN)):
            acc = terms(own, chunks, (run + dx * 8 + dy * 2) * RUN + n, acc)
        acc = lax.fori_loop(
            0, kept, lambda n, acc: terms(own, chunks, extra_near[n], acc), acc
        )
        for g in range(GROUPS):
            for n, a in enumerate(acc[g]):
                sums[slot, n, pl.ds(at + 8 * g, 8), :] = a
        return 0

    lax.fori_loop(0, (live + IROWS - 1) // IROWS, rows_step, 0)


def gathered(sums, slot, number):
    out = []
    diagonal = lanes_of() - lax.broadcasted_iota(jnp.int32, (8, LANES), 0)
    for n in range(number):
        total = jnp.zeros((8, LANES), jnp.float32)
        for k in range(LANES // 8):
            part = jnp.sum(sums[slot, n, 8 * k : 8 * k + 8, :], axis=1, keepdims=True)
            total = jnp.where(diagonal == 8 * k, part, total)
        out.append(jnp.sum(total, axis=0, keepdims=True))
    return out


def note_extra(run, extra_first, extra_near):
    kept = jnp.int32(0)
    for dx, dy in itertools.product((-1, 0, 1), repeat=2):
        beside = run + dx * 8 + dy * 2
        first = extra_first[beside]

        def note(k, _, first=first, kept=kept):
            extra_near[kept + k] = RUNS * RUN + first + k
            return 0

        number = extra_first[beside + 1] - first
        lax.fori_loop(0, number, note, 0)
        kept = kept + number
    return kept


def sweep(shift, units, meta, chunks, columns, sums, extra_first, extra_near, force, terms, finish):
    fields, number = (5, 3) if force else (4, 1)
    longest = pack(shift, units, meta, chunks, extra_first, force)
    owns = []
    most = jnp.int32(0)
    for index in range(8):
        cell, octant, moves, _ = own_octant(index, shift, meta)
        first, live = meta[cell, octant], meta[cell, octant + 16]
        most = jnp.maximum(most, live)
        chunk = own_chunk(units, cell, first, live, moves, force)
        store_columns(columns, index, chunk, fields)
        owns.append((cell, first, live, chunk))

    def octant_step(index, _):
        cell, octant, _, run = own_octant(index, shift, meta)
        live = jnp.minimum(meta[cell, octant + 16], LANES)
        kept = lax.cond(
            longest > RUN * LANES,
            lambda: note_extra(run, extra_first, extra_near),
            lambda: jnp.int32(0),
        )
        sweep_rows(index, run, live, kept, chunks, columns, sums, extra_near, fields, terms)
        return 0

    lax.fori_loop(0, 8, octant_step, 0)
    for index, (cell, first, live, chunk) in enumerate(owns):
        finish(cell, first, jnp.minimum(live, LANES), gathered(sums, index, number), chunk)

    @pl.when(most > LANES)
    def _():
        def octant_rest(index, _):
            cell, octant, moves, run = own_octant(index, shift, meta)
            moves = [real(v) for v in moves]
            first, live = meta[cell, octant], meta[cell, octant + 16]
            kept = lax.cond(
                longest > RUN * LANES,
                lambda: note_extra(run, extra_first, extra_near),
                lambda: jnp.int32(0),
            )

            def part_step(part, _):
                done = part * LANES
                chunk = own_chunk(units, cell, first + done, live - done, moves, force)
                store_columns(columns, 0, chunk, fields)
                here = jnp.minimum(live - done, LANES)
                sweep_rows(0, run, here, kept, chunks, columns, sums, extra_near, fields, terms)
                finish(cell, first + done, here, gathered(sums, 0, number), chunk)
                return 0

            lax.fori_loop(1, (live + LANES - 1) // LANES, part_step, 0)
            return 0

        lax.fori_loop(0, 8, octant_rest, 0)


def put(ref, first, count, rows):
    block = jnp.minimum(first // LANES, BLOCKS - 1)
    later = jnp.minimum(block + 1, BLOCKS - 1)
    turn = first % LANES
    turned = pltpu.roll(rows, turn, 1)
    lane = lanes_of(rows.shape)
    ref[block] = jnp.where((lane >= turn) & (lane < turn + count), turned, ref[block])
    ref[later] = jnp.where(lane < turn + count - LANES, turned, ref[later])


def distance(own, x, y, z):
    dx, dy, dz = own[0] - x, own[1] - y, own[2] - z
    d2 = dx * dx + dy * dy + dz * dz
    return dx, dy, dz, d2 * lax.rsqrt(jnp.maximum(d2, 1e-30))


def added(acc, terms):
    return terms if acc is None else tuple(a + t for a, t in zip(acc, terms))


def density_terms(own, chunks, at, acc):
    x, y, z, m = (chunks[at, f] for f in range(4))
    out = []
    for g in range(GROUPS):
        dist = distance(own[g], x, y, z)[3]
        rest = jnp.maximum(1.0 - dist * own[g][3], 0.0)
        rest2 = rest * rest
        out.append(added(acc[g], ((rest2 * rest2) * (1.25 - rest) * m,)))
    return out


def force_terms(own, chunks, at, acc):
    x, y, z, m, c, k = (chunks[at, f] for f in range(6))
    out = []
    for g in range(GROUPS):
        dx, dy, dz, dist = distance(own[g], x, y, z)
        rest_own = jnp.maximum(own[g][3] - dist * own[g][4], 0.0)
        rest_far = jnp.maximum(c - dist * k, 0.0)
        coef = m * (rest_own * rest_own * rest_own) + rest_far * rest_far * rest_far
        out.append(added(acc[g], (coef * dx, coef * dy, coef * dz)))
    return out


def read_counts(units, meta, counts, sem, cells):
    for cell in range(cells):
        counts[cell : cell + 1] = units[cell, 0, ROW_META : ROW_META + 1, :].astype(jnp.int32)
    copy = pltpu.make_async_copy(counts, meta, sem)
    copy.start()
    copy.wait()


def density_kernel(
    units, c_ref, meta, counts, chunks, columns, sums, extra_first, extra_near, sem
):
    read_counts(units, meta, counts, sem, 8)
    for cell in range(8):
        c_ref[cell] = units[cell, :, ROW_C : ROW_C + 1, :]

    def finish(cell, first, count, result, chunk):
        ih = chunk[3:4]
        rho = (4.0 * KW) * result[0] * (ih * ih * ih)
        c = cbrt(chunk[5:6] * inv_cbrt(jnp.maximum(rho, 1e-30)))
        put(c_ref.at[cell], first, count, c)

    sweep(
        0, units, meta, chunks, columns, sums, extra_first, extra_near, False, density_terms, finish
    )


def force_kernel(
    units, hot_ref, old_ref, act_ref, dens_ref, acc_ref,
    meta, counts, chunks, columns, sums, extra_first, extra_near, sem, found,
):
    read_counts(units, meta, counts, sem, 27)
    found[...] = jnp.zeros_like(found)

    def finish(cell, first, count, result, chunk):
        put(found, first, count, jnp.concatenate(result + [result[0]] * 5, axis=0))

    sweep(
        1, units, meta, chunks, columns, sums, extra_first, extra_near, True, force_terms, finish
    )
    row = lax.broadcasted_iota(jnp.int32, (8, LANES), 0)
    parts = []
    for k in range(BLOCKS):
        c = units[13, k, ROW_C : ROW_C + 1, :]
        ratio = units[13, k, 5:6, :] / (c * c * c)
        parts.append(jnp.where(row == 3, ratio * ratio * ratio, found[k] * KG))
    back = jnp.dot(
        split3(jnp.concatenate(parts, axis=1)), hot_ref[...],
        preferred_element_type=jnp.float32,
    )
    back = join3(back)
    live = act_ref[...] == 1
    for axis in range(3):
        acc_ref[axis] = jnp.where(live, back[axis : axis + 1], 0.0)
    dens_ref[...] = jnp.where(live, back[3:4], old_ref[...])


def run_density(units):
    return pl.pallas_call(
        density_kernel,
        out_shape=shape(8, BLOCKS, 1, LANES),
        in_specs=vmem(1),
        out_specs=vmem(1)[0],
        scratch_shapes=scratch(8, 96, 4, 1),
        compiler_params=grant(12),
        name="density",
    )(units)


def run_force(units, hot, old, act):
    return pl.pallas_call(
        force_kernel,
        out_shape=(shape(1, COUNT), shape(3, 1, COUNT)),
        in_specs=vmem(4),
        out_specs=tuple(vmem(2)),
        scratch_shapes=scratch(27, 324, 6, 3) + [pltpu.VMEM((BLOCKS, 8, LANES), jnp.float32)],
        compiler_params=grant(24),
        name="force",
    )(units, hot, old, act)


def vmem(n):
    return [pl.BlockSpec(memory_space=pltpu.VMEM)] * n


def grant(mib):
    return pltpu.CompilerParams(vmem_limit_bytes=mib * 1024 * 1024)


def scratch(cells, extra, rows, number):
    return [
        pltpu.SMEM((cells, LANES), jnp.int32),
        pltpu.VMEM((cells, LANES), jnp.int32),
        pltpu.VMEM((RUNS * RUN + extra, rows, 8, LANES), jnp.float32),
        pltpu.VMEM((8, 5, LANES, LANES), jnp.float32),
        pltpu.VMEM((8, number, LANES, LANES), jnp.float32),
        pltpu.SMEM((RUNS + 1,), jnp.int32),
        pltpu.SMEM((extra + 1,), jnp.int32),
        pltpu.SemaphoreType.DMA,
    ]


def shape(*dims):
    return jax.ShapeDtypeStruct(dims, jnp.float32)


def from_next(block, axis):
    count = lax.axis_size(axis)
    return lax.ppermute(block, axis, [(i, (i - 1) % count) for i in range(count)])


def from_last(block, axis):
    count = lax.axis_size(axis)
    return lax.ppermute(block, axis, [(i, (i + 1) % count) for i in range(count)])


def body(positions, smoothing, masses, entropy, old_density, active):
    row = lambda a: a.reshape(1, COUNT)
    unit, hot = pl.pallas_call(
        sort_kernel,
        out_shape=(shape(BLOCKS, 8, LANES), jax.ShapeDtypeStruct((COUNT, COUNT), jnp.bfloat16)),
        in_specs=vmem(6),
        out_specs=tuple(vmem(2)),
        compiler_params=grant(8),
        name="sort_octants",
    )(
        positions.reshape(3, 1, COUNT), row(smoothing), row(masses), row(entropy), row(old_density),
        row(active),
    )
    units = unit[None, None, None]
    for dim, axis in ((0, "gx"), (1, "gy"), (2, "gz")):
        units = jnp.concatenate([units, from_next(units, axis)], axis=dim)
    c = run_density(units.reshape(8, BLOCKS, 8, LANES)).reshape(2, 2, 2, BLOCKS, 1, LANES)
    units = jnp.concatenate([units[..., :ROW_C, :], c, units[..., ROW_C + 1 :, :]], axis=-2)
    for dim, axis in ((0, "gx"), (1, "gy"), (2, "gz")):
        low = lax.slice_in_dim(units, 0, 1, axis=dim)
        high = lax.slice_in_dim(units, 1, 2, axis=dim)
        c = slice(ROW_C, ROW_C + 1)
        far = from_last(
            jnp.concatenate([low[..., :5, :], high[..., c, :], low[..., ROW_C:, :]], axis=-2), axis
        )
        upper = low[..., dim : dim + 1, :] >= 0.5
        low_c = jnp.where(upper, low[..., c, :], far[..., 5:6, :])
        low = jnp.concatenate([low[..., :ROW_C, :], low_c, low[..., ROW_C + 1 :, :]], axis=-2)
        units = jnp.concatenate([far, low, high], axis=dim)
    dens, accel = run_force(
        units.reshape(27, BLOCKS, 8, LANES), hot, row(old_density), row(active)
    )
    return dens.reshape(1, 1, 1, COUNT), accel.reshape(1, 1, 1, 3, COUNT)


def solution(mesh):
    cells = P("gx", "gy", "gz", None)
    vectors = P("gx", "gy", "gz", None, None)
    return jax.shard_map(
        body,
        mesh=mesh,
        in_specs=(vectors, cells, cells, cells, cells, cells),
        out_specs=(cells, vectors),
        check_vma=False,
    )
```

```python
import itertools
import math

import jax
import jax.numpy as jnp
from jax import lax
from jax.experimental import pallas as pl
from jax.experimental.pallas import tpu as pltpu
from jax.sharding import PartitionSpec as P

KW = 21.0 / (2.0 * math.pi)
KG = 210.0 / math.pi
LANES = 128
COUNT = 768
BLOCKS = COUNT // LANES
FAR = 1.0e4
IROWS = 16
GROUPS = IROWS // 8
PART = 96
RUN = 3
RUNS = 32
ROW_C = 6
ROW_META = 7


def cbrt(x):
    return jnp.exp(jnp.log(x) * (1.0 / 3.0))


def inv_cbrt(x):
    return jnp.exp(jnp.log(x) * (-1.0 / 3.0))


def parts3(rows):
    hi = rows.astype(jnp.bfloat16).astype(jnp.float32)
    rest = rows - hi
    mid = rest.astype(jnp.bfloat16).astype(jnp.float32)
    return jnp.concatenate([hi, mid, rest - mid, jnp.zeros_like(hi)], axis=0)


def split3(rows):
    return parts3(rows).astype(jnp.bfloat16)


def join3(parts):
    return parts[0:8] + parts[8:16] + parts[16:24]


def one_hot_of(rank):
    place = lax.broadcasted_iota(jnp.int32, (COUNT, COUNT), 0)
    return (place == rank).astype(jnp.float32).astype(jnp.bfloat16)


def sort_kernel(*refs):
    arguments, (unit_ref, hot_ref), held, sem = refs[:6], refs[6:8], refs[8:14], refs[14]
    copies = [
        pltpu.make_async_copy(source, target, sem.at[k])
        for k, (source, target) in enumerate(zip(arguments, held))
    ]
    for copy in copies:
        copy.start()
    for copy in copies:
        copy.wait()
    pos_ref, h_ref, m_ref, a_ref, old_ref, act_ref = held
    x, y, z = pos_ref[0], pos_ref[1], pos_ref[2]
    ih = 1.0 / h_ref[...]
    ih2 = ih * ih
    mass = m_ref[...]
    b = mass * a_ref[...] * (ih2 * ih2 * ih)
    c = cbrt(b * inv_cbrt(old_ref[...]))
    one, zero = jnp.int32(1), jnp.int32(0)
    key = (
        jnp.where(x >= 0.5, 8 * one, zero)
        + jnp.where(y >= 0.5, 4 * one, zero)
        + jnp.where(z >= 0.5, 2 * one, zero)
        + jnp.where(act_ref[...] == 1, zero, one)
    )
    kind = lax.broadcasted_iota(jnp.int32, (16, COUNT), 0)
    hot = (kind == key).astype(jnp.float32)
    blocks = jnp.concatenate([hot[:, k * LANES : (k + 1) * LANES] for k in range(BLOCKS)], axis=0)
    before = lax.broadcasted_iota(jnp.int32, (LANES, LANES), 0)
    after = lax.broadcasted_iota(jnp.int32, (LANES, LANES), 1)
    upper = (before < after).astype(jnp.float32).astype(jnp.bfloat16)
    prefix = jnp.dot(blocks.astype(jnp.bfloat16), upper, preferred_element_type=jnp.float32)
    sums = [jnp.sum(hot[:, k * LANES : (k + 1) * LANES], axis=1, keepdims=True) for k in range(BLOCKS)]
    running = jnp.zeros((16, 1), jnp.float32)
    carried = []
    for k in range(BLOCKS):
        carried.append(prefix[16 * k : 16 * (k + 1)] + running)
        running = running + sums[k]
    total = jnp.broadcast_to(running, (16, LANES))
    start = jnp.zeros((16, LANES), jnp.float32)
    row = lax.broadcasted_iota(jnp.int32, (16, LANES), 0)
    for k in range(15):
        start = start + jnp.where(row > k, total[k : k + 1], 0.0)
    rank = jnp.concatenate(
        [
            jnp.sum(
                hot[:, k * LANES : (k + 1) * LANES] * (carried[k] + start), axis=0, keepdims=True
            )
            for k in range(BLOCKS)
        ],
        axis=1,
    ).astype(jnp.int32)
    moves = one_hot_of(rank)
    hot_ref[...] = moves
    rows = jnp.concatenate([x, y, z, ih, mass, b, c, jnp.zeros_like(c)], axis=0)
    moved = lax.dot_general(
        split3(rows), moves, (((1,), (1,)), ((), ())), preferred_element_type=jnp.float32
    )
    moved = join3(moved)
    lane = lax.broadcasted_iota(jnp.int32, (16, LANES), 1)
    even = (row & 1) == 0
    octant = row >> 1
    counts = (
        jnp.where((lane == octant) & even, start, 0.0)
        + jnp.where(lane == octant + 8, total, 0.0)
        + jnp.where((lane == octant + 16) & even, total, 0.0)
    )
    counts = jnp.sum(counts, axis=0, keepdims=True)
    which = lax.broadcasted_iota(jnp.int32, (8, LANES), 0)
    for k in range(BLOCKS):
        unit_ref[k] = jnp.where(which == ROW_META, counts, moved[:, k * LANES : (k + 1) * LANES])


def real(value):
    return jnp.float32(value) if isinstance(value, int) else value.astype(jnp.float32)


def lanes_of(shape=(8, LANES)):
    return lax.broadcasted_iota(jnp.int32, shape, len(shape) - 1)


def windows(units, cell, first, number):
    block, turn = first >> 7, first & (LANES - 1)
    back = (LANES - turn) & (LANES - 1)
    turned = [
        pltpu.roll(units[cell, jnp.clip(block + k, 0, BLOCKS - 1)], back, 1)
        for k in range(number + 1)
    ]
    keep = lanes_of() < LANES - turn
    return [jnp.where(keep, turned[k], turned[k + 1]) for k in range(number)]


def moved_by(chunk, moves):
    row = lax.broadcasted_iota(jnp.int32, (8, LANES), 0)
    step = jnp.float32(0.0)
    for axis in range(3):
        step = jnp.where(row == axis, jnp.float32(moves[axis]), step)
    return chunk + step


def cell_of(cx, cy, cz, shift):
    side = 2 + shift
    return (cx * side + cy) * side + cz


def run_parts(gx, gy, side, shift, meta):
    ex, ey = gx + shift, gy + shift
    cx, cy = ex // 2, ey // 2
    octant = (ex % 2) * 4 + (ey % 2) * 2
    last = jnp.int32(side == shift) if isinstance(side, int) else (side == shift).astype(jnp.int32)
    parts = []
    for which in range(2):
        cz = which + (side if shift else 0)
        half = last if which else 1 - last
        cell = cell_of(cx, cy, cz, shift)
        first_octant = octant + (0 if which else half)
        first = meta[cell, first_octant]
        count = meta[cell, first_octant + 8]
        count = count + jnp.where(half == 1, 0, meta[cell, octant + 9])
        parts.append((cell, first, count, (cx, cy, cz)))
    return parts


def run_chunks(units, parts, begin, number, force):
    (cell_a, first_a, count_a, moves_a), (cell_b, first_b, count_b, moves_b) = parts
    a = windows(units, cell_a, first_a + begin, number)
    b = windows(units, cell_b, first_b + begin - count_a, number)
    out = []
    for k in range(number):
        lane = lanes_of() + (begin + k * LANES)
        chunk = jnp.where(lane < count_a, moved_by(a[k], moves_a), moved_by(b[k], moves_b))
        chunk = jnp.where(lane < count_a + count_b, chunk, FAR)
        x, y, z, ih, m, c = (chunk[f : f + 1] for f in (0, 1, 2, 3, 4, ROW_C))
        out.append((x, y, z, m, c, c * ih) if force else (x, y, z, m))
    return out


def store_chunk(chunks, at, rows):
    for f, values in enumerate(rows):
        chunks[at, f] = jnp.broadcast_to(values, (8, LANES))


def pack(shift, units, meta, chunks, extra_first, force):
    longest = jnp.int32(0)
    for gx, gy, side in itertools.product(range(4), range(4), range(2)):
        run = (gx * 4 + gy) * 2 + side
        parts = run_parts(gx, gy, side, shift, meta)
        longest = jnp.maximum(longest, parts[0][2] + parts[1][2])
        for k, rows in enumerate(run_chunks(units, parts, jnp.int32(0), RUN, force)):
            store_chunk(chunks, run * RUN + k, rows)

    @pl.when(longest > RUN * LANES)
    def _():
        def long_run(run, used):
            parts = run_parts(run // 8, run // 2 % 4, run % 2, shift, meta)
            parts = [(c, f, n, [real(v) for v in mv]) for c, f, n, mv in parts]
            more = jnp.maximum((parts[0][2] + parts[1][2] + LANES - 1) // LANES - RUN, 0)
            extra_first[run] = used

            def one(k, _):
                rows = run_chunks(units, parts, (k + RUN) * LANES, 1, force)[0]
                store_chunk(chunks, RUNS * RUN + used + k, rows)
                return 0

            lax.fori_loop(0, more, one, 0)
            return used + more

        extra_first[RUNS] = lax.fori_loop(0, RUNS, long_run, jnp.int32(0))

    return longest


def own_octant(index, shift, meta):
    ix, iy, iz = index // 4, index // 2 % 2, index % 2
    if shift:
        moves, octant = (1, 1, 1), index
    else:
        moves, octant = (ix, iy, iz), 7 - index
    cell = cell_of(*moves, shift)
    run = ((1 + ix) * 4 + 1 + iy) * 2 + iz
    return cell, octant, moves, run


def own_chunk(units, cell, first, live, moves, force):
    chunk = moved_by(windows(units, cell, first, 1)[0], moves)
    if force:
        c = chunk[ROW_C : ROW_C + 1] / cbrt(chunk[4:5])
        chunk = jnp.concatenate([chunk[0:3], c, c * chunk[3:4], chunk[5:8]], axis=0)
    return jnp.where(lanes_of() < live, chunk, FAR)


def store_columns(columns, slot, chunk, fields):
    part = lax.broadcasted_iota(jnp.int32, (32, fields * LANES), 0)
    field = lax.broadcasted_iota(jnp.int32, (32, fields * LANES), 1) // LANES
    pick = ((part & 7) == field) & (part < 24)
    values = jnp.dot(
        parts3(chunk).T[:PART].astype(jnp.bfloat16), pick.astype(jnp.float32).astype(jnp.bfloat16),
        preferred_element_type=jnp.float32,
    )
    for f in range(fields):
        columns[slot, f] = values[:PART, f * LANES : (f + 1) * LANES]


def sweep_rows(slot, run, live, kept, chunks, columns, sums, extra_near, fields, terms):
    def rows_step(k, _):
        at = pl.multiple_of(k * IROWS, IROWS)
        own = [
            [columns[slot, f, pl.ds(at + 8 * g, 8), :] for f in range(fields)]
            for g in range(GROUPS)
        ]
        acc = [None] * GROUPS
        for dx, dy, n in itertools.product((-1, 0, 1), (-1, 0, 1), range(RUN)):
            acc = terms(own, chunks, (run + dx * 8 + dy * 2) * RUN + n, acc)
        acc = lax.fori_loop(
            0, kept, lambda n, acc: terms(own, chunks, extra_near[n], acc), acc
        )
        for g in range(GROUPS):
            for n, a in enumerate(acc[g]):
                sums[slot, n, pl.ds(at + 8 * g, 8), :] = a
        return 0

    lax.fori_loop(0, (live + IROWS - 1) // IROWS, rows_step, 0)


def gathered(sums, slot, number):
    out = []
    diagonal = lanes_of() - lax.broadcasted_iota(jnp.int32, (8, LANES), 0)
    for n in range(number):
        total = jnp.zeros((8, LANES), jnp.float32)
        for k in range(PART // 8):
            part = jnp.sum(sums[slot, n, 8 * k : 8 * k + 8, :], axis=1, keepdims=True)
            total = jnp.where(diagonal == 8 * k, part, total)
        out.append(jnp.sum(total, axis=0, keepdims=True))
    return out


def note_extra(run, extra_first, extra_near):
    kept = jnp.int32(0)
    for dx, dy in itertools.product((-1, 0, 1), repeat=2):
        beside = run + dx * 8 + dy * 2
        first = extra_first[beside]

        def note(k, _, first=first, kept=kept):
            extra_near[kept + k] = RUNS * RUN + first + k
            return 0

        number = extra_first[beside + 1] - first
        lax.fori_loop(0, number, note, 0)
        kept = kept + number
    return kept


def sweep(shift, units, meta, chunks, columns, sums, extra_first, extra_near, force, terms, finish):
    fields, number = (5, 3) if force else (4, 1)
    longest = pack(shift, units, meta, chunks, extra_first, force)
    owns = []
    most = jnp.int32(0)
    for index in range(8):
        cell, octant, moves, _ = own_octant(index, shift, meta)
        first, live = meta[cell, octant], meta[cell, octant + 16]
        most = jnp.maximum(most, live)
        chunk = own_chunk(units, cell, first, live, moves, force)
        store_columns(columns, index, chunk, fields)
        owns.append((cell, first, live, chunk))

    def octant_step(index, _):
        cell, octant, _, run = own_octant(index, shift, meta)
        live = jnp.minimum(meta[cell, octant + 16], PART)
        kept = lax.cond(
            longest > RUN * LANES,
            lambda: note_extra(run, extra_first, extra_near),
            lambda: jnp.int32(0),
        )
        sweep_rows(index, run, live, kept, chunks, columns, sums, extra_near, fields, terms)
        return 0

    lax.fori_loop(0, 8, octant_step, 0)
    for index, (cell, first, live, chunk) in enumerate(owns):
        finish(cell, first, jnp.minimum(live, PART), gathered(sums, index, number), chunk)

    @pl.when(most > PART)
    def _():
        def octant_rest(index, _):
            cell, octant, moves, run = own_octant(index, shift, meta)
            moves = [real(v) for v in moves]
            first, live = meta[cell, octant], meta[cell, octant + 16]
            kept = lax.cond(
                longest > RUN * LANES,
                lambda: note_extra(run, extra_first, extra_near),
                lambda: jnp.int32(0),
            )

            def part_step(part, _):
                done = part * PART
                chunk = own_chunk(units, cell, first + done, live - done, moves, force)
                store_columns(columns, 0, chunk, fields)
                here = jnp.minimum(live - done, PART)
                sweep_rows(0, run, here, kept, chunks, columns, sums, extra_near, fields, terms)
                finish(cell, first + done, here, gathered(sums, 0, number), chunk)
                return 0

            lax.fori_loop(1, (live + PART - 1) // PART, part_step, 0)
            return 0

        lax.fori_loop(0, 8, octant_rest, 0)


def put(ref, first, count, rows):
    block = jnp.minimum(first // LANES, BLOCKS - 1)
    later = jnp.minimum(block + 1, BLOCKS - 1)
    turn = first % LANES
    turned = pltpu.roll(rows, turn, 1)
    lane = lanes_of(rows.shape)
    ref[block] = jnp.where((lane >= turn) & (lane < turn + count), turned, ref[block])
    ref[later] = jnp.where(lane < turn + count - LANES, turned, ref[later])


def distance(own, x, y, z):
    dx, dy, dz = own[0] - x, own[1] - y, own[2] - z
    d2 = dx * dx + dy * dy + dz * dz
    return dx, dy, dz, d2 * lax.rsqrt(jnp.maximum(d2, 1e-30))


def added(acc, terms):
    return terms if acc is None else tuple(a + t for a, t in zip(acc, terms))


def density_terms(own, chunks, at, acc):
    x, y, z, m = (chunks[at, f] for f in range(4))
    out = []
    for g in range(GROUPS):
        dist = distance(own[g], x, y, z)[3]
        rest = jnp.maximum(1.0 - dist * own[g][3], 0.0)
        rest2 = rest * rest
        out.append(added(acc[g], ((rest2 * rest2) * (1.25 - rest) * m,)))
    return out


def force_terms(own, chunks, at, acc):
    x, y, z, m, c, k = (chunks[at, f] for f in range(6))
    out = []
    for g in range(GROUPS):
        dx, dy, dz, dist = distance(own[g], x, y, z)
        rest_own = jnp.maximum(own[g][3] - dist * own[g][4], 0.0)
        rest_far = jnp.maximum(c - dist * k, 0.0)
        coef = m * (rest_own * rest_own * rest_own) + rest_far * rest_far * rest_far
        out.append(added(acc[g], (coef * dx, coef * dy, coef * dz)))
    return out


def read_counts(units, meta, counts, sem, cells):
    for cell in range(cells):
        counts[cell : cell + 1] = units[cell, 0, ROW_META : ROW_META + 1, :].astype(jnp.int32)
    copy = pltpu.make_async_copy(counts, meta, sem)
    copy.start()
    copy.wait()


def density_kernel(
    units, c_ref, meta, counts, chunks, columns, sums, extra_first, extra_near, sem
):
    read_counts(units, meta, counts, sem, 8)
    for cell in range(8):
        c_ref[cell] = units[cell, :, ROW_C : ROW_C + 1, :]

    def finish(cell, first, count, result, chunk):
        ih = chunk[3:4]
        rho = (4.0 * KW) * result[0] * (ih * ih * ih)
        c = cbrt(chunk[5:6] * inv_cbrt(jnp.maximum(rho, 1e-30)))
        put(c_ref.at[cell], first, count, c)

    sweep(
        0, units, meta, chunks, columns, sums, extra_first, extra_near, False, density_terms, finish
    )


def force_kernel(
    units, hot_ref, old_ref, act_ref, dens_ref, acc_ref,
    meta, counts, chunks, columns, sums, extra_first, extra_near, sem, found,
):
    read_counts(units, meta, counts, sem, 27)
    found[...] = jnp.zeros_like(found)

    def finish(cell, first, count, result, chunk):
        put(found, first, count, jnp.concatenate(result + [result[0]] * 5, axis=0))

    sweep(
        1, units, meta, chunks, columns, sums, extra_first, extra_near, True, force_terms, finish
    )
    row = lax.broadcasted_iota(jnp.int32, (8, LANES), 0)
    parts = []
    for k in range(BLOCKS):
        c = units[13, k, ROW_C : ROW_C + 1, :]
        ratio = units[13, k, 5:6, :] / (c * c * c)
        parts.append(jnp.where(row == 3, ratio * ratio * ratio, found[k] * KG))
    back = jnp.dot(
        split3(jnp.concatenate(parts, axis=1)), hot_ref[...],
        preferred_element_type=jnp.float32,
    )
    back = join3(back)
    live = act_ref[...] == 1
    for axis in range(3):
        acc_ref[axis] = jnp.where(live, back[axis : axis + 1], 0.0)
    dens_ref[...] = jnp.where(live, back[3:4], old_ref[...])


def run_density(units):
    return pl.pallas_call(
        density_kernel,
        out_shape=shape(8, BLOCKS, 1, LANES),
        in_specs=vmem(1),
        out_specs=vmem(1)[0],
        scratch_shapes=scratch(8, 96, 4, 1),
        compiler_params=grant(12),
        name="density",
    )(units)


def run_force(units, hot, old, act):
    return pl.pallas_call(
        force_kernel,
        out_shape=(shape(1, COUNT), shape(3, 1, COUNT)),
        in_specs=vmem(4),
        out_specs=tuple(vmem(2)),
        scratch_shapes=scratch(27, 324, 6, 3) + [pltpu.VMEM((BLOCKS, 8, LANES), jnp.float32)],
        compiler_params=grant(24),
        name="force",
    )(units, hot, old, act)


def vmem(n):
    return [pl.BlockSpec(memory_space=pltpu.VMEM)] * n


def grant(mib):
    return pltpu.CompilerParams(vmem_limit_bytes=mib * 1024 * 1024)


def scratch(cells, extra, rows, number):
    return [
        pltpu.SMEM((cells, LANES), jnp.int32),
        pltpu.VMEM((cells, LANES), jnp.int32),
        pltpu.VMEM((RUNS * RUN + extra, rows, 8, LANES), jnp.float32),
        pltpu.VMEM((8, 5, PART, LANES), jnp.float32),
        pltpu.VMEM((8, number, PART, LANES), jnp.float32),
        pltpu.SMEM((RUNS + 1,), jnp.int32),
        pltpu.SMEM((extra + 1,), jnp.int32),
        pltpu.SemaphoreType.DMA,
    ]


def shape(*dims):
    return jax.ShapeDtypeStruct(dims, jnp.float32)


def from_next(block, axis):
    count = lax.axis_size(axis)
    return lax.ppermute(block, axis, [(i, (i - 1) % count) for i in range(count)])


def from_last(block, axis):
    count = lax.axis_size(axis)
    return lax.ppermute(block, axis, [(i, (i + 1) % count) for i in range(count)])


def body(positions, smoothing, masses, entropy, old_density, active):
    row = lambda a: a.reshape(1, COUNT)
    unit, hot = pl.pallas_call(
        sort_kernel,
        out_shape=(shape(BLOCKS, 8, LANES), jax.ShapeDtypeStruct((COUNT, COUNT), jnp.bfloat16)),
        in_specs=[pl.BlockSpec(memory_space=pltpu.HBM)] * 6,
        out_specs=tuple(vmem(2)),
        scratch_shapes=[pltpu.VMEM((3, 1, COUNT), jnp.float32)]
        + [pltpu.VMEM((1, COUNT), jnp.float32)] * 4
        + [pltpu.VMEM((1, COUNT), jnp.int32), pltpu.SemaphoreType.DMA((6,))],
        compiler_params=grant(8),
        name="sort_octants",
    )(
        positions.reshape(3, 1, COUNT), row(smoothing), row(masses), row(entropy), row(old_density),
        row(active),
    )
    units = unit[None, None, None]
    for dim, axis in ((0, "gx"), (1, "gy"), (2, "gz")):
        units = jnp.concatenate([units, from_next(units, axis)], axis=dim)
    c = run_density(units.reshape(8, BLOCKS, 8, LANES)).reshape(2, 2, 2, BLOCKS, 1, LANES)
    units = jnp.concatenate([units[..., :ROW_C, :], c, units[..., ROW_C + 1 :, :]], axis=-2)
    for dim, axis in ((0, "gx"), (1, "gy"), (2, "gz")):
        low = lax.slice_in_dim(units, 0, 1, axis=dim)
        high = lax.slice_in_dim(units, 1, 2, axis=dim)
        c = slice(ROW_C, ROW_C + 1)
        far = from_last(
            jnp.concatenate([low[..., :5, :], high[..., c, :], low[..., ROW_C:, :]], axis=-2), axis
        )
        upper = low[..., dim : dim + 1, :] >= 0.5
        low_c = jnp.where(upper, low[..., c, :], far[..., 5:6, :])
        low = jnp.concatenate([low[..., :ROW_C, :], low_c, low[..., ROW_C + 1 :, :]], axis=-2)
        units = jnp.concatenate([far, low, high], axis=dim)
    dens, accel = run_force(
        units.reshape(27, BLOCKS, 8, LANES), hot, row(old_density), row(active)
    )
    return dens.reshape(1, 1, 1, COUNT), accel.reshape(1, 1, 1, 3, COUNT)


def solution(mesh):
    cells = P("gx", "gy", "gz", None)
    vectors = P("gx", "gy", "gz", None, None)
    return jax.shard_map(
        body,
        mesh=mesh,
        in_specs=(vectors, cells, cells, cells, cells, cells),
        out_specs=(cells, vectors),
        check_vma=False,
    )
```

```python
import itertools
import math

import jax
import jax.numpy as jnp
from jax import lax
from jax.experimental import pallas as pl
from jax.experimental.pallas import tpu as pltpu
from jax.sharding import PartitionSpec as P

KW = 21.0 / (2.0 * math.pi)
KG = 210.0 / math.pi
LANES = 128
COUNT = 768
BLOCKS = COUNT // LANES
FAR = 1.0e4
IROWS = 16
GROUPS = IROWS // 8
PART = 96
RUN = 3
RUNS = 32
ROW_C = 6
ROW_META = 7


def cbrt(x):
    return jnp.exp(jnp.log(x) * (1.0 / 3.0))


def inv_cbrt(x):
    return jnp.exp(jnp.log(x) * (-1.0 / 3.0))


def parts3(rows):
    hi = rows.astype(jnp.bfloat16).astype(jnp.float32)
    rest = rows - hi
    mid = rest.astype(jnp.bfloat16).astype(jnp.float32)
    return jnp.concatenate([hi, mid, rest - mid, jnp.zeros_like(hi)], axis=0)


def split3(rows):
    return parts3(rows).astype(jnp.bfloat16)


def join3(parts):
    return parts[0:8] + parts[8:16] + parts[16:24]


def one_hot_of(rank):
    place = lax.broadcasted_iota(jnp.int32, (COUNT, COUNT), 0)
    return (place == rank).astype(jnp.float32).astype(jnp.bfloat16)


def sort_kernel(rows_ref, unit_ref, hot_ref):
    x, y, z, h, mass, gas, old, live = (rows_ref[k : k + 1] for k in range(8))
    ih = 1.0 / h
    ih2 = ih * ih
    b = mass * gas * (ih2 * ih2 * ih)
    c = cbrt(b * inv_cbrt(old))
    one, zero = jnp.int32(1), jnp.int32(0)
    key = (
        jnp.where(x >= 0.5, 8 * one, zero)
        + jnp.where(y >= 0.5, 4 * one, zero)
        + jnp.where(z >= 0.5, 2 * one, zero)
        + jnp.where(live == 1.0, zero, one)
    )
    kind = lax.broadcasted_iota(jnp.int32, (16, COUNT), 0)
    hot = (kind == key).astype(jnp.float32)
    blocks = jnp.concatenate([hot[:, k * LANES : (k + 1) * LANES] for k in range(BLOCKS)], axis=0)
    before = lax.broadcasted_iota(jnp.int32, (LANES, LANES), 0)
    after = lax.broadcasted_iota(jnp.int32, (LANES, LANES), 1)
    upper = (before < after).astype(jnp.float32).astype(jnp.bfloat16)
    prefix = jnp.dot(blocks.astype(jnp.bfloat16), upper, preferred_element_type=jnp.float32)
    sums = [jnp.sum(hot[:, k * LANES : (k + 1) * LANES], axis=1, keepdims=True) for k in range(BLOCKS)]
    running = jnp.zeros((16, 1), jnp.float32)
    carried = []
    for k in range(BLOCKS):
        carried.append(prefix[16 * k : 16 * (k + 1)] + running)
        running = running + sums[k]
    total = jnp.broadcast_to(running, (16, LANES))
    start = jnp.zeros((16, LANES), jnp.float32)
    row = lax.broadcasted_iota(jnp.int32, (16, LANES), 0)
    for k in range(15):
        start = start + jnp.where(row > k, total[k : k + 1], 0.0)
    rank = jnp.concatenate(
        [
            jnp.sum(
                hot[:, k * LANES : (k + 1) * LANES] * (carried[k] + start), axis=0, keepdims=True
            )
            for k in range(BLOCKS)
        ],
        axis=1,
    ).astype(jnp.int32)
    moves = one_hot_of(rank)
    hot_ref[...] = moves
    rows = jnp.concatenate([x, y, z, ih, mass, b, c, jnp.zeros_like(c)], axis=0)
    moved = lax.dot_general(
        split3(rows), moves, (((1,), (1,)), ((), ())), preferred_element_type=jnp.float32
    )
    moved = join3(moved)
    lane = lax.broadcasted_iota(jnp.int32, (16, LANES), 1)
    even = (row & 1) == 0
    octant = row >> 1
    counts = (
        jnp.where((lane == octant) & even, start, 0.0)
        + jnp.where(lane == octant + 8, total, 0.0)
        + jnp.where((lane == octant + 16) & even, total, 0.0)
    )
    counts = jnp.sum(counts, axis=0, keepdims=True)
    which = lax.broadcasted_iota(jnp.int32, (8, LANES), 0)
    for k in range(BLOCKS):
        unit_ref[k] = jnp.where(which == ROW_META, counts, moved[:, k * LANES : (k + 1) * LANES])


def real(value):
    return jnp.float32(value) if isinstance(value, int) else value.astype(jnp.float32)


def lanes_of(shape=(8, LANES)):
    return lax.broadcasted_iota(jnp.int32, shape, len(shape) - 1)


def windows(units, cell, first, number):
    block, turn = first >> 7, first & (LANES - 1)
    back = (LANES - turn) & (LANES - 1)
    turned = [
        pltpu.roll(units[cell, jnp.clip(block + k, 0, BLOCKS - 1)], back, 1)
        for k in range(number + 1)
    ]
    keep = lanes_of() < LANES - turn
    return [jnp.where(keep, turned[k], turned[k + 1]) for k in range(number)]


def moved_by(chunk, moves):
    row = lax.broadcasted_iota(jnp.int32, (8, LANES), 0)
    step = jnp.float32(0.0)
    for axis in range(3):
        step = jnp.where(row == axis, real(moves[axis]), step)
    return chunk + step


def cell_of(cx, cy, cz, shift):
    side = 2 + shift
    return (cx * side + cy) * side + cz


def run_parts(gx, gy, side, shift, meta):
    ex, ey = gx + shift, gy + shift
    cx, cy = ex // 2, ey // 2
    octant = (ex % 2) * 4 + (ey % 2) * 2
    last = jnp.int32(side == shift) if isinstance(side, int) else (side == shift).astype(jnp.int32)
    parts = []
    for which in range(2):
        cz = which + (side if shift else 0)
        half = last if which else 1 - last
        cell = cell_of(cx, cy, cz, shift)
        first_octant = octant + (0 if which else half)
        first = meta[cell, first_octant]
        count = meta[cell, first_octant + 8]
        count = count + jnp.where(half == 1, 0, meta[cell, octant + 9])
        parts.append((cell, first, count, (cx - shift, cy - shift, cz - shift)))
    return parts


def run_chunks(units, parts, begin, number, force):
    (cell_a, first_a, count_a, moves_a), (cell_b, first_b, count_b, moves_b) = parts
    a = windows(units, cell_a, first_a + begin, number)
    b = windows(units, cell_b, first_b + begin - count_a, number)
    out = []
    for k in range(number):
        lane = lanes_of() + (begin + k * LANES)
        chunk = jnp.where(lane < count_a, moved_by(a[k], moves_a), moved_by(b[k], moves_b))
        chunk = jnp.where(lane < count_a + count_b, chunk, FAR)
        x, y, z, ih, m, c = (chunk[f : f + 1] for f in (0, 1, 2, 3, 4, ROW_C))
        out.append((x, y, z, m, c, c * ih) if force else (x, y, z, m))
    return out


def store_chunk(chunks, at, rows):
    for f, values in enumerate(rows):
        chunks[at, f] = jnp.broadcast_to(values, (8, LANES))


def pack(shift, units, meta, chunks, extra_first, force):
    longest = jnp.int32(0)
    for gx, gy, side in itertools.product(range(4), range(4), range(2)):
        run = (gx * 4 + gy) * 2 + side
        parts = run_parts(gx, gy, side, shift, meta)
        longest = jnp.maximum(longest, parts[0][2] + parts[1][2])
        for k, rows in enumerate(run_chunks(units, parts, jnp.int32(0), RUN, force)):
            store_chunk(chunks, run * RUN + k, rows)

    @pl.when(longest > RUN * LANES)
    def _():
        def long_run(run, used):
            parts = run_parts(run // 8, run // 2 % 4, run % 2, shift, meta)
            parts = [(c, f, n, [real(v) for v in mv]) for c, f, n, mv in parts]
            more = jnp.maximum((parts[0][2] + parts[1][2] + LANES - 1) // LANES - RUN, 0)
            extra_first[run] = used

            def one(k, _):
                rows = run_chunks(units, parts, (k + RUN) * LANES, 1, force)[0]
                store_chunk(chunks, RUNS * RUN + used + k, rows)
                return 0

            lax.fori_loop(0, more, one, 0)
            return used + more

        extra_first[RUNS] = lax.fori_loop(0, RUNS, long_run, jnp.int32(0))

    return longest


def own_octant(index, shift, meta):
    ix, iy, iz = index // 4, index // 2 % 2, index % 2
    if shift:
        place, octant = (1, 1, 1), index
    else:
        place, octant = (ix, iy, iz), 7 - index
    cell = cell_of(*place, shift)
    moves = [p - shift for p in place]
    run = ((1 + ix) * 4 + 1 + iy) * 2 + iz
    return cell, octant, moves, run


def own_chunk(units, cell, first, live, moves, force):
    chunk = moved_by(windows(units, cell, first, 1)[0], moves)
    if force:
        c = chunk[ROW_C : ROW_C + 1] / cbrt(chunk[4:5])
        chunk = jnp.concatenate([chunk[0:3], c, c * chunk[3:4], chunk[5:8]], axis=0)
    return jnp.where(lanes_of() < live, chunk, FAR)


def store_columns(columns, slot, chunk, fields):
    part = lax.broadcasted_iota(jnp.int32, (32, fields * LANES), 0)
    field = lax.broadcasted_iota(jnp.int32, (32, fields * LANES), 1) // LANES
    pick = ((part & 7) == field) & (part < 24)
    values = jnp.dot(
        parts3(chunk).T[:PART].astype(jnp.bfloat16), pick.astype(jnp.float32).astype(jnp.bfloat16),
        preferred_element_type=jnp.float32,
    )
    for f in range(fields):
        columns[slot, f] = values[:PART, f * LANES : (f + 1) * LANES]


def sweep_rows(slot, run, live, kept, chunks, columns, sums, extra_near, fields, terms):
    def rows_step(k, _):
        at = pl.multiple_of(k * IROWS, IROWS)
        own = [
            [columns[slot, f, pl.ds(at + 8 * g, 8), :] for f in range(fields)]
            for g in range(GROUPS)
        ]
        acc = [None] * GROUPS
        for dx, dy, n in itertools.product((-1, 0, 1), (-1, 0, 1), range(RUN)):
            acc = terms(own, chunks, (run + dx * 8 + dy * 2) * RUN + n, acc)
        acc = lax.fori_loop(
            0, kept, lambda n, acc: terms(own, chunks, extra_near[n], acc), acc
        )
        for g in range(GROUPS):
            for n, a in enumerate(acc[g]):
                sums[slot, n, pl.ds(at + 8 * g, 8), :] = a
        return 0

    lax.fori_loop(0, (live + IROWS - 1) // IROWS, rows_step, 0)


def gathered(sums, slot, number):
    out = []
    diagonal = lanes_of() - lax.broadcasted_iota(jnp.int32, (8, LANES), 0)
    for n in range(number):
        total = jnp.zeros((8, LANES), jnp.float32)
        for k in range(PART // 8):
            part = jnp.sum(sums[slot, n, 8 * k : 8 * k + 8, :], axis=1, keepdims=True)
            total = jnp.where(diagonal == 8 * k, part, total)
        out.append(jnp.sum(total, axis=0, keepdims=True))
    return out


def note_extra(run, extra_first, extra_near):
    kept = jnp.int32(0)
    for dx, dy in itertools.product((-1, 0, 1), repeat=2):
        beside = run + dx * 8 + dy * 2
        first = extra_first[beside]

        def note(k, _, first=first, kept=kept):
            extra_near[kept + k] = RUNS * RUN + first + k
            return 0

        number = extra_first[beside + 1] - first
        lax.fori_loop(0, number, note, 0)
        kept = kept + number
    return kept


def sweep(shift, units, meta, chunks, columns, sums, extra_first, extra_near, force, terms, finish):
    fields, number = (5, 3) if force else (4, 1)
    longest = pack(shift, units, meta, chunks, extra_first, force)
    owns = []
    most = jnp.int32(0)
    for index in range(8):
        cell, octant, moves, _ = own_octant(index, shift, meta)
        first, live = meta[cell, octant], meta[cell, octant + 16]
        most = jnp.maximum(most, live)
        chunk = own_chunk(units, cell, first, live, moves, force)
        store_columns(columns, index, chunk, fields)
        owns.append((cell, first, live, chunk))

    def octant_step(index, _):
        cell, octant, _, run = own_octant(index, shift, meta)
        live = jnp.minimum(meta[cell, octant + 16], PART)
        kept = lax.cond(
            longest > RUN * LANES,
            lambda: note_extra(run, extra_first, extra_near),
            lambda: jnp.int32(0),
        )
        sweep_rows(index, run, live, kept, chunks, columns, sums, extra_near, fields, terms)
        return 0

    lax.fori_loop(0, 8, octant_step, 0)
    for index, (cell, first, live, chunk) in enumerate(owns):
        finish(cell, first, jnp.minimum(live, PART), gathered(sums, index, number), chunk)

    @pl.when(most > PART)
    def _():
        def octant_rest(index, _):
            cell, octant, moves, run = own_octant(index, shift, meta)
            moves = [real(v) for v in moves]
            first, live = meta[cell, octant], meta[cell, octant + 16]
            kept = lax.cond(
                longest > RUN * LANES,
                lambda: note_extra(run, extra_first, extra_near),
                lambda: jnp.int32(0),
            )

            def part_step(part, _):
                done = part * PART
                chunk = own_chunk(units, cell, first + done, live - done, moves, force)
                store_columns(columns, 0, chunk, fields)
                here = jnp.minimum(live - done, PART)
                sweep_rows(0, run, here, kept, chunks, columns, sums, extra_near, fields, terms)
                finish(cell, first + done, here, gathered(sums, 0, number), chunk)
                return 0

            lax.fori_loop(1, (live + PART - 1) // PART, part_step, 0)
            return 0

        lax.fori_loop(0, 8, octant_rest, 0)


def put(ref, first, count, rows):
    block = jnp.minimum(first // LANES, BLOCKS - 1)
    later = jnp.minimum(block + 1, BLOCKS - 1)
    turn = first % LANES
    turned = pltpu.roll(rows, turn, 1)
    lane = lanes_of(rows.shape)
    ref[block] = jnp.where((lane >= turn) & (lane < turn + count), turned, ref[block])
    ref[later] = jnp.where(lane < turn + count - LANES, turned, ref[later])


def distance(own, x, y, z):
    dx, dy, dz = own[0] - x, own[1] - y, own[2] - z
    d2 = dx * dx + dy * dy + dz * dz
    return dx, dy, dz, d2 * lax.rsqrt(jnp.maximum(d2, 1e-30))


def added(acc, terms):
    return terms if acc is None else tuple(a + t for a, t in zip(acc, terms))


def density_terms(own, chunks, at, acc):
    x, y, z, m = (chunks[at, f] for f in range(4))
    out = []
    for g in range(GROUPS):
        dist = distance(own[g], x, y, z)[3]
        rest = jnp.maximum(1.0 - dist * own[g][3], 0.0)
        rest2 = rest * rest
        out.append(added(acc[g], ((rest2 * rest2) * (1.25 - rest) * m,)))
    return out


def force_terms(own, chunks, at, acc):
    x, y, z, m, c, k = (chunks[at, f] for f in range(6))
    out = []
    for g in range(GROUPS):
        dx, dy, dz, dist = distance(own[g], x, y, z)
        rest_own = jnp.maximum(own[g][3] - dist * own[g][4], 0.0)
        rest_far = jnp.maximum(c - dist * k, 0.0)
        coef = m * (rest_own * rest_own * rest_own) + rest_far * rest_far * rest_far
        out.append(added(acc[g], (coef * dx, coef * dy, coef * dz)))
    return out


def read_counts(units, meta, counts, sem, cells):
    for cell in range(cells):
        counts[cell : cell + 1] = units[cell, 0, ROW_META : ROW_META + 1, :].astype(jnp.int32)
    copy = pltpu.make_async_copy(counts, meta, sem)
    copy.start()
    copy.wait()


def density_kernel(
    units, c_ref, meta, counts, chunks, columns, sums, extra_first, extra_near, sem
):
    read_counts(units, meta, counts, sem, 8)
    for cell in range(8):
        c_ref[cell] = units[cell, :, ROW_C : ROW_C + 1, :]

    def finish(cell, first, count, result, chunk):
        ih = chunk[3:4]
        rho = (4.0 * KW) * result[0] * (ih * ih * ih)
        c = cbrt(chunk[5:6] * inv_cbrt(jnp.maximum(rho, 1e-30)))
        put(c_ref.at[cell], first, count, c)

    sweep(
        0, units, meta, chunks, columns, sums, extra_first, extra_near, False, density_terms, finish
    )


def force_kernel(
    units, hot_ref, old_ref, act_ref, dens_ref, acc_ref,
    meta, counts, chunks, columns, sums, extra_first, extra_near, sem, found,
):
    read_counts(units, meta, counts, sem, 27)
    found[...] = jnp.zeros_like(found)

    def finish(cell, first, count, result, chunk):
        put(found, first, count, jnp.concatenate(result + [result[0]] * 5, axis=0))

    sweep(
        1, units, meta, chunks, columns, sums, extra_first, extra_near, True, force_terms, finish
    )
    row = lax.broadcasted_iota(jnp.int32, (8, LANES), 0)
    parts = []
    for k in range(BLOCKS):
        c = units[13, k, ROW_C : ROW_C + 1, :]
        ratio = units[13, k, 5:6, :] / (c * c * c)
        parts.append(jnp.where(row == 3, ratio * ratio * ratio, found[k] * KG))
    back = jnp.dot(
        split3(jnp.concatenate(parts, axis=1)), hot_ref[...],
        preferred_element_type=jnp.float32,
    )
    back = join3(back)
    live = act_ref[...] == 1
    for axis in range(3):
        acc_ref[axis] = jnp.where(live, back[axis : axis + 1], 0.0)
    dens_ref[...] = jnp.where(live, back[3:4], old_ref[...])


def run_density(units):
    return pl.pallas_call(
        density_kernel,
        out_shape=shape(8, BLOCKS, 1, LANES),
        in_specs=vmem(1),
        out_specs=vmem(1)[0],
        scratch_shapes=scratch(8, 96, 4, 1),
        compiler_params=grant(12),
        name="density",
    )(units)


def run_force(units, hot, old, act):
    return pl.pallas_call(
        force_kernel,
        out_shape=(shape(1, COUNT), shape(3, 1, COUNT)),
        in_specs=vmem(4),
        out_specs=tuple(vmem(2)),
        scratch_shapes=scratch(27, 324, 6, 3) + [pltpu.VMEM((BLOCKS, 8, LANES), jnp.float32)],
        compiler_params=grant(24),
        name="force",
    )(units, hot, old, act)


def vmem(n):
    return [pl.BlockSpec(memory_space=pltpu.VMEM)] * n


def grant(mib):
    return pltpu.CompilerParams(vmem_limit_bytes=mib * 1024 * 1024)


def scratch(cells, extra, rows, number):
    return [
        pltpu.SMEM((cells, LANES), jnp.int32),
        pltpu.VMEM((cells, LANES), jnp.int32),
        pltpu.VMEM((RUNS * RUN + extra, rows, 8, LANES), jnp.float32),
        pltpu.VMEM((8, 5, PART, LANES), jnp.float32),
        pltpu.VMEM((8, number, PART, LANES), jnp.float32),
        pltpu.SMEM((RUNS + 1,), jnp.int32),
        pltpu.SMEM((extra + 1,), jnp.int32),
        pltpu.SemaphoreType.DMA,
    ]


def shape(*dims):
    return jax.ShapeDtypeStruct(dims, jnp.float32)


def from_next(block, axis):
    count = lax.axis_size(axis)
    return lax.ppermute(block, axis, [(i, (i - 1) % count) for i in range(count)])


def from_last(block, axis):
    count = lax.axis_size(axis)
    return lax.ppermute(block, axis, [(i, (i + 1) % count) for i in range(count)])


def body(positions, smoothing, masses, entropy, old_density, active):
    row = lambda a: a.reshape(1, COUNT)
    unit, hot = pl.pallas_call(
        sort_kernel,
        out_shape=(shape(BLOCKS, 8, LANES), jax.ShapeDtypeStruct((COUNT, COUNT), jnp.bfloat16)),
        in_specs=vmem(1),
        out_specs=tuple(vmem(2)),
        compiler_params=grant(8),
        name="sort_octants",
    )(
        jnp.concatenate(
            [
                positions.reshape(3, COUNT), row(smoothing), row(masses), row(entropy),
                row(old_density), row(active).astype(jnp.float32),
            ],
            axis=0,
        )
    )
    units = unit[None, None, None]
    for dim, axis in ((0, "gx"), (1, "gy"), (2, "gz")):
        units = jnp.concatenate([units, from_next(units, axis)], axis=dim)
    c = run_density(units.reshape(8, BLOCKS, 8, LANES)).reshape(2, 2, 2, BLOCKS, 1, LANES)
    units = jnp.concatenate([units[..., :ROW_C, :], c, units[..., ROW_C + 1 :, :]], axis=-2)
    for dim, axis in ((0, "gx"), (1, "gy"), (2, "gz")):
        low = lax.slice_in_dim(units, 0, 1, axis=dim)
        high = lax.slice_in_dim(units, 1, 2, axis=dim)
        c = slice(ROW_C, ROW_C + 1)
        far = from_last(
            jnp.concatenate([low[..., :5, :], high[..., c, :], low[..., ROW_C:, :]], axis=-2), axis
        )
        upper = low[..., dim : dim + 1, :] >= 0.5
        low_c = jnp.where(upper, low[..., c, :], far[..., 5:6, :])
        low = jnp.concatenate([low[..., :ROW_C, :], low_c, low[..., ROW_C + 1 :, :]], axis=-2)
        units = jnp.concatenate([far, low, high], axis=dim)
    dens, accel = run_force(
        units.reshape(27, BLOCKS, 8, LANES), hot, row(old_density), row(active)
    )
    return dens.reshape(1, 1, 1, COUNT), accel.reshape(1, 1, 1, 3, COUNT)


def solution(mesh):
    cells = P("gx", "gy", "gz", None)
    vectors = P("gx", "gy", "gz", None, None)
    return jax.shard_map(
        body,
        mesh=mesh,
        in_specs=(vectors, cells, cells, cells, cells, cells),
        out_specs=(cells, vectors),
        check_vma=False,
    )
```

```python
import itertools
import math

import jax
import jax.numpy as jnp
from jax import lax
from jax.experimental import pallas as pl
from jax.experimental.pallas import tpu as pltpu
from jax.sharding import PartitionSpec as P

KW = 21.0 / (2.0 * math.pi)
KG = 210.0 / math.pi
LANES = 128
COUNT = 768
BLOCKS = COUNT // LANES
FAR = 1.0e4
IROWS = 16
GROUPS = IROWS // 8
PART = 96
RUN = 3
RUNS = 32
ROW_C = 6
ROW_META = 7


def cbrt(x):
    return jnp.exp(jnp.log(x) * (1.0 / 3.0))


def inv_cbrt(x):
    return jnp.exp(jnp.log(x) * (-1.0 / 3.0))


def parts3(rows):
    hi = rows.astype(jnp.bfloat16).astype(jnp.float32)
    rest = rows - hi
    mid = rest.astype(jnp.bfloat16).astype(jnp.float32)
    return jnp.concatenate([hi, mid, rest - mid, jnp.zeros_like(hi)], axis=0)


def split3(rows):
    return parts3(rows).astype(jnp.bfloat16)


def join3(parts):
    return parts[0:8] + parts[8:16] + parts[16:24]


def one_hot_of(rank):
    place = lax.broadcasted_iota(jnp.int32, (COUNT, COUNT), 0)
    return (place == rank).astype(jnp.float32).astype(jnp.bfloat16)


def sort_kernel(rows_ref, unit_ref, hot_ref):
    x, y, z, h, mass, gas, old, live = (rows_ref[k : k + 1] for k in range(8))
    ih = 1.0 / h
    ih2 = ih * ih
    b = mass * gas * (ih2 * ih2 * ih)
    c = cbrt(b * inv_cbrt(old))
    one, zero = jnp.int32(1), jnp.int32(0)
    key = (
        jnp.where(x >= 0.5, 8 * one, zero)
        + jnp.where(y >= 0.5, 4 * one, zero)
        + jnp.where(z >= 0.5, 2 * one, zero)
        + jnp.where(live == 1.0, zero, one)
    )
    kind = lax.broadcasted_iota(jnp.int32, (16, COUNT), 0)
    hot = (kind == key).astype(jnp.float32)
    blocks = jnp.concatenate([hot[:, k * LANES : (k + 1) * LANES] for k in range(BLOCKS)], axis=0)
    before = lax.broadcasted_iota(jnp.int32, (LANES, LANES), 0)
    after = lax.broadcasted_iota(jnp.int32, (LANES, LANES), 1)
    upper = (before < after).astype(jnp.float32).astype(jnp.bfloat16)
    prefix = jnp.dot(blocks.astype(jnp.bfloat16), upper, preferred_element_type=jnp.float32)
    sums = [jnp.sum(hot[:, k * LANES : (k + 1) * LANES], axis=1, keepdims=True) for k in range(BLOCKS)]
    running = jnp.zeros((16, 1), jnp.float32)
    carried = []
    for k in range(BLOCKS):
        carried.append(prefix[16 * k : 16 * (k + 1)] + running)
        running = running + sums[k]
    total = jnp.broadcast_to(running, (16, LANES))
    start = jnp.zeros((16, LANES), jnp.float32)
    row = lax.broadcasted_iota(jnp.int32, (16, LANES), 0)
    for k in range(15):
        start = start + jnp.where(row > k, total[k : k + 1], 0.0)
    rank = jnp.concatenate(
        [
            jnp.sum(
                hot[:, k * LANES : (k + 1) * LANES] * (carried[k] + start), axis=0, keepdims=True
            )
            for k in range(BLOCKS)
        ],
        axis=1,
    ).astype(jnp.int32)
    moves = one_hot_of(rank)
    hot_ref[...] = moves
    rows = jnp.concatenate([x, y, z, ih, mass, b, c, jnp.zeros_like(c)], axis=0)
    moved = lax.dot_general(
        split3(rows), moves, (((1,), (1,)), ((), ())), preferred_element_type=jnp.float32
    )
    moved = join3(moved)
    lane = lax.broadcasted_iota(jnp.int32, (16, LANES), 1)
    even = (row & 1) == 0
    octant = row >> 1
    counts = (
        jnp.where((lane == octant) & even, start, 0.0)
        + jnp.where(lane == octant + 8, total, 0.0)
        + jnp.where((lane == octant + 16) & even, total, 0.0)
    )
    counts = jnp.sum(counts, axis=0, keepdims=True)
    which = lax.broadcasted_iota(jnp.int32, (8, LANES), 0)
    for k in range(BLOCKS):
        unit_ref[k] = jnp.where(which == ROW_META, counts, moved[:, k * LANES : (k + 1) * LANES])


def real(value):
    return jnp.float32(value) if isinstance(value, int) else value.astype(jnp.float32)


def lanes_of(shape=(8, LANES)):
    return lax.broadcasted_iota(jnp.int32, shape, len(shape) - 1)


def windows(units, cell, first, number):
    block, turn = first >> 7, first & (LANES - 1)
    back = (LANES - turn) & (LANES - 1)
    turned = [
        pltpu.roll(units[cell, jnp.clip(block + k, 0, BLOCKS - 1)], back, 1)
        for k in range(number + 1)
    ]
    keep = lanes_of() < LANES - turn
    return [jnp.where(keep, turned[k], turned[k + 1]) for k in range(number)]


def moved_by(chunk, moves):
    row = lax.broadcasted_iota(jnp.int32, (8, LANES), 0)
    step = jnp.float32(0.0)
    for axis in range(3):
        step = jnp.where(row == axis, real(moves[axis]), step)
    return chunk + step


def cell_of(cx, cy, cz, shift):
    side = 2 + shift
    return (cx * side + cy) * side + cz


def run_parts(gx, gy, side, shift, meta):
    ex, ey = gx + shift, gy + shift
    cx, cy = ex // 2, ey // 2
    octant = (ex % 2) * 4 + (ey % 2) * 2
    last = jnp.int32(side == shift) if isinstance(side, int) else (side == shift).astype(jnp.int32)
    parts = []
    for which in range(2):
        cz = which + (side if shift else 0)
        half = last if which else 1 - last
        cell = cell_of(cx, cy, cz, shift)
        first_octant = octant + (0 if which else half)
        first = meta[cell, first_octant]
        count = meta[cell, first_octant + 8]
        count = count + jnp.where(half == 1, 0, meta[cell, octant + 9])
        parts.append((cell, first, count, (cx - shift, cy - shift, cz - shift)))
    return parts


def run_chunks(units, parts, begin, number, force):
    (cell_a, first_a, count_a, moves_a), (cell_b, first_b, count_b, moves_b) = parts
    a = windows(units, cell_a, first_a + begin, number)
    b = windows(units, cell_b, first_b + begin - count_a, number)
    out = []
    for k in range(number):
        lane = lanes_of() + (begin + k * LANES)
        chunk = jnp.where(lane < count_a, moved_by(a[k], moves_a), moved_by(b[k], moves_b))
        chunk = jnp.where(lane < count_a + count_b, chunk, FAR)
        x, y, z, ih, m, c = (chunk[f : f + 1] for f in (0, 1, 2, 3, 4, ROW_C))
        out.append((x, y, z, m, c, c * ih) if force else (x, y, z, m))
    return out


def store_chunk(chunks, at, rows):
    for f, values in enumerate(rows):
        chunks[at, f] = jnp.broadcast_to(values, (8, LANES))


def pack(shift, units, meta, chunks, extra_first, force):
    longest = jnp.int32(0)
    for gx, gy, side in itertools.product(range(4), range(4), range(2)):
        run = (gx * 4 + gy) * 2 + side
        parts = run_parts(gx, gy, side, shift, meta)
        longest = jnp.maximum(longest, parts[0][2] + parts[1][2])
        for k, rows in enumerate(run_chunks(units, parts, jnp.int32(0), RUN, force)):
            store_chunk(chunks, run * RUN + k, rows)

    @pl.when(longest > RUN * LANES)
    def _():
        def long_run(run, used):
            parts = run_parts(run // 8, run // 2 % 4, run % 2, shift, meta)
            parts = [(c, f, n, [real(v) for v in mv]) for c, f, n, mv in parts]
            more = jnp.maximum((parts[0][2] + parts[1][2] + LANES - 1) // LANES - RUN, 0)
            extra_first[run] = used

            def one(k, _):
                rows = run_chunks(units, parts, (k + RUN) * LANES, 1, force)[0]
                store_chunk(chunks, RUNS * RUN + used + k, rows)
                return 0

            lax.fori_loop(0, more, one, 0)
            return used + more

        extra_first[RUNS] = lax.fori_loop(0, RUNS, long_run, jnp.int32(0))

    return longest


def own_octant(index, shift, meta):
    ix, iy, iz = index // 4, index // 2 % 2, index % 2
    if shift:
        place, octant = (1, 1, 1), index
    else:
        place, octant = (ix, iy, iz), 7 - index
    cell = cell_of(*place, shift)
    moves = [p - shift for p in place]
    run = ((1 + ix) * 4 + 1 + iy) * 2 + iz
    return cell, octant, moves, run


def own_chunk(units, cell, first, live, moves, force):
    chunk = moved_by(windows(units, cell, first, 1)[0], moves)
    if force:
        c = chunk[ROW_C : ROW_C + 1] / cbrt(chunk[4:5])
        chunk = jnp.concatenate([chunk[0:3], c, c * chunk[3:4], chunk[5:8]], axis=0)
    return jnp.where(lanes_of() < live, chunk, FAR)


def store_columns(columns, slot, chunk, fields):
    part = lax.broadcasted_iota(jnp.int32, (32, fields * LANES), 0)
    field = lax.broadcasted_iota(jnp.int32, (32, fields * LANES), 1) // LANES
    pick = ((part & 7) == field) & (part < 24)
    values = jnp.dot(
        parts3(chunk).T[:PART].astype(jnp.bfloat16), pick.astype(jnp.float32).astype(jnp.bfloat16),
        preferred_element_type=jnp.float32,
    )
    for f in range(fields):
        columns[slot, f] = values[:PART, f * LANES : (f + 1) * LANES]


def sweep_rows(slot, run, live, kept, chunks, columns, sums, extra_near, fields, terms):
    def rows_step(k, _):
        at = pl.multiple_of(k * IROWS, IROWS)
        own = [
            [columns[slot, f, pl.ds(at + 8 * g, 8), :] for f in range(fields)]
            for g in range(GROUPS)
        ]
        acc = [None] * GROUPS
        for dx, dy, n in itertools.product((-1, 0, 1), (-1, 0, 1), range(RUN)):
            acc = terms(own, chunks, (run + dx * 8 + dy * 2) * RUN + n, acc)
        acc = lax.fori_loop(
            0, kept, lambda n, acc: terms(own, chunks, extra_near[n], acc), acc
        )
        for g in range(GROUPS):
            for n, a in enumerate(acc[g]):
                sums[slot, n, pl.ds(at + 8 * g, 8), :] = a
        return 0

    lax.fori_loop(0, (live + IROWS - 1) // IROWS, rows_step, 0)


def gathered(sums, slot, number):
    out = []
    diagonal = lanes_of() - lax.broadcasted_iota(jnp.int32, (8, LANES), 0)
    for n in range(number):
        if number > 1:
            turned = jnp.sum(sums[slot, n].T, axis=0, keepdims=True)
            rest = jnp.zeros((1, LANES - PART), jnp.float32)
            out.append(jnp.concatenate([turned, rest], axis=1))
            continue
        total = jnp.zeros((8, LANES), jnp.float32)
        for k in range(PART // 8):
            part = jnp.sum(sums[slot, n, 8 * k : 8 * k + 8, :], axis=1, keepdims=True)
            total = jnp.where(diagonal == 8 * k, part, total)
        out.append(jnp.sum(total, axis=0, keepdims=True))
    return out


def note_extra(run, extra_first, extra_near):
    kept = jnp.int32(0)
    for dx, dy in itertools.product((-1, 0, 1), repeat=2):
        beside = run + dx * 8 + dy * 2
        first = extra_first[beside]

        def note(k, _, first=first, kept=kept):
            extra_near[kept + k] = RUNS * RUN + first + k
            return 0

        number = extra_first[beside + 1] - first
        lax.fori_loop(0, number, note, 0)
        kept = kept + number
    return kept


def sweep(shift, units, meta, chunks, columns, sums, extra_first, extra_near, force, terms, finish):
    fields, number = (5, 3) if force else (4, 1)
    longest = pack(shift, units, meta, chunks, extra_first, force)
    owns = []
    most = jnp.int32(0)
    for index in range(8):
        cell, octant, moves, _ = own_octant(index, shift, meta)
        first, live = meta[cell, octant], meta[cell, octant + 16]
        most = jnp.maximum(most, live)
        chunk = own_chunk(units, cell, first, live, moves, force)
        store_columns(columns, index, chunk, fields)
        owns.append((cell, first, live, chunk))

    def octant_step(index, _):
        cell, octant, _, run = own_octant(index, shift, meta)
        live = jnp.minimum(meta[cell, octant + 16], PART)
        kept = lax.cond(
            longest > RUN * LANES,
            lambda: note_extra(run, extra_first, extra_near),
            lambda: jnp.int32(0),
        )
        sweep_rows(index, run, live, kept, chunks, columns, sums, extra_near, fields, terms)
        return 0

    lax.fori_loop(0, 8, octant_step, 0)
    for index, (cell, first, live, chunk) in enumerate(owns):
        finish(cell, first, jnp.minimum(live, PART), gathered(sums, index, number), chunk)

    @pl.when(most > PART)
    def _():
        def octant_rest(index, _):
            cell, octant, moves, run = own_octant(index, shift, meta)
            moves = [real(v) for v in moves]
            first, live = meta[cell, octant], meta[cell, octant + 16]
            kept = lax.cond(
                longest > RUN * LANES,
                lambda: note_extra(run, extra_first, extra_near),
                lambda: jnp.int32(0),
            )

            def part_step(part, _):
                done = part * PART
                chunk = own_chunk(units, cell, first + done, live - done, moves, force)
                store_columns(columns, 0, chunk, fields)
                here = jnp.minimum(live - done, PART)
                sweep_rows(0, run, here, kept, chunks, columns, sums, extra_near, fields, terms)
                finish(cell, first + done, here, gathered(sums, 0, number), chunk)
                return 0

            lax.fori_loop(1, (live + PART - 1) // PART, part_step, 0)
            return 0

        lax.fori_loop(0, 8, octant_rest, 0)


def put(ref, first, count, rows):
    block = jnp.minimum(first // LANES, BLOCKS - 1)
    later = jnp.minimum(block + 1, BLOCKS - 1)
    turn = first % LANES
    turned = pltpu.roll(rows, turn, 1)
    lane = lanes_of(rows.shape)
    ref[block] = jnp.where((lane >= turn) & (lane < turn + count), turned, ref[block])
    ref[later] = jnp.where(lane < turn + count - LANES, turned, ref[later])


def distance(own, x, y, z):
    dx, dy, dz = own[0] - x, own[1] - y, own[2] - z
    d2 = dx * dx + dy * dy + dz * dz
    return dx, dy, dz, d2 * lax.rsqrt(jnp.maximum(d2, 1e-30))


def added(acc, terms):
    return terms if acc is None else tuple(a + t for a, t in zip(acc, terms))


def density_terms(own, chunks, at, acc):
    x, y, z, m = (chunks[at, f] for f in range(4))
    out = []
    for g in range(GROUPS):
        dist = distance(own[g], x, y, z)[3]
        rest = jnp.maximum(1.0 - dist * own[g][3], 0.0)
        rest2 = rest * rest
        out.append(added(acc[g], ((rest2 * rest2) * (1.25 - rest) * m,)))
    return out


def force_terms(own, chunks, at, acc):
    x, y, z, m, c, k = (chunks[at, f] for f in range(6))
    out = []
    for g in range(GROUPS):
        dx, dy, dz, dist = distance(own[g], x, y, z)
        rest_own = jnp.maximum(own[g][3] - dist * own[g][4], 0.0)
        rest_far = jnp.maximum(c - dist * k, 0.0)
        coef = m * (rest_own * rest_own * rest_own) + rest_far * rest_far * rest_far
        out.append(added(acc[g], (coef * dx, coef * dy, coef * dz)))
    return out


def read_counts(units, meta, counts, sem, cells):
    for cell in range(cells):
        counts[cell : cell + 1] = units[cell, 0, ROW_META : ROW_META + 1, :].astype(jnp.int32)
    copy = pltpu.make_async_copy(counts, meta, sem)
    copy.start()
    copy.wait()


def density_kernel(
    units, c_ref, meta, counts, chunks, columns, sums, extra_first, extra_near, sem
):
    read_counts(units, meta, counts, sem, 8)
    for cell in range(8):
        c_ref[cell] = units[cell, :, ROW_C : ROW_C + 1, :]

    def finish(cell, first, count, result, chunk):
        ih = chunk[3:4]
        rho = (4.0 * KW) * result[0] * (ih * ih * ih)
        c = cbrt(chunk[5:6] * inv_cbrt(jnp.maximum(rho, 1e-30)))
        put(c_ref.at[cell], first, count, c)

    sweep(
        0, units, meta, chunks, columns, sums, extra_first, extra_near, False, density_terms, finish
    )


def force_kernel(
    units, hot_ref, old_ref, act_ref, dens_ref, acc_ref,
    meta, counts, chunks, columns, sums, extra_first, extra_near, sem, found,
):
    read_counts(units, meta, counts, sem, 27)
    found[...] = jnp.zeros_like(found)

    def finish(cell, first, count, result, chunk):
        put(found, first, count, jnp.concatenate(result + [result[0]] * 5, axis=0))

    sweep(
        1, units, meta, chunks, columns, sums, extra_first, extra_near, True, force_terms, finish
    )
    row = lax.broadcasted_iota(jnp.int32, (8, LANES), 0)
    parts = []
    for k in range(BLOCKS):
        c = units[13, k, ROW_C : ROW_C + 1, :]
        ratio = units[13, k, 5:6, :] / (c * c * c)
        parts.append(jnp.where(row == 3, ratio * ratio * ratio, found[k] * KG))
    back = jnp.dot(
        split3(jnp.concatenate(parts, axis=1)), hot_ref[...],
        preferred_element_type=jnp.float32,
    )
    back = join3(back)
    live = act_ref[...] == 1
    for axis in range(3):
        acc_ref[axis] = jnp.where(live, back[axis : axis + 1], 0.0)
    dens_ref[...] = jnp.where(live, back[3:4], old_ref[...])


def run_density(units):
    return pl.pallas_call(
        density_kernel,
        out_shape=shape(8, BLOCKS, 1, LANES),
        in_specs=vmem(1),
        out_specs=vmem(1)[0],
        scratch_shapes=scratch(8, 96, 4, 1),
        compiler_params=grant(12),
        name="density",
    )(units)


def run_force(units, hot, old, act):
    return pl.pallas_call(
        force_kernel,
        out_shape=(shape(1, COUNT), shape(3, 1, COUNT)),
        in_specs=vmem(4),
        out_specs=tuple(vmem(2)),
        scratch_shapes=scratch(27, 324, 6, 3) + [pltpu.VMEM((BLOCKS, 8, LANES), jnp.float32)],
        compiler_params=grant(24),
        name="force",
    )(units, hot, old, act)


def vmem(n):
    return [pl.BlockSpec(memory_space=pltpu.VMEM)] * n


def grant(mib):
    return pltpu.CompilerParams(vmem_limit_bytes=mib * 1024 * 1024)


def scratch(cells, extra, rows, number):
    return [
        pltpu.SMEM((cells, LANES), jnp.int32),
        pltpu.VMEM((cells, LANES), jnp.int32),
        pltpu.VMEM((RUNS * RUN + extra, rows, 8, LANES), jnp.float32),
        pltpu.VMEM((8, 5, PART, LANES), jnp.float32),
        pltpu.VMEM((8, number, PART, LANES), jnp.float32),
        pltpu.SMEM((RUNS + 1,), jnp.int32),
        pltpu.SMEM((extra + 1,), jnp.int32),
        pltpu.SemaphoreType.DMA,
    ]


def shape(*dims):
    return jax.ShapeDtypeStruct(dims, jnp.float32)


def from_next(block, axis):
    count = lax.axis_size(axis)
    return lax.ppermute(block, axis, [(i, (i - 1) % count) for i in range(count)])


def from_last(block, axis):
    count = lax.axis_size(axis)
    return lax.ppermute(block, axis, [(i, (i + 1) % count) for i in range(count)])


def body(positions, smoothing, masses, entropy, old_density, active):
    row = lambda a: a.reshape(1, COUNT)
    unit, hot = pl.pallas_call(
        sort_kernel,
        out_shape=(shape(BLOCKS, 8, LANES), jax.ShapeDtypeStruct((COUNT, COUNT), jnp.bfloat16)),
        in_specs=vmem(1),
        out_specs=tuple(vmem(2)),
        compiler_params=grant(8),
        name="sort_octants",
    )(
        jnp.concatenate(
            [
                positions.reshape(3, COUNT), row(smoothing), row(masses), row(entropy),
                row(old_density), row(active).astype(jnp.float32),
            ],
            axis=0,
        )
    )
    units = unit[None, None, None]
    for dim, axis in ((0, "gx"), (1, "gy"), (2, "gz")):
        units = jnp.concatenate([units, from_next(units, axis)], axis=dim)
    c = run_density(units.reshape(8, BLOCKS, 8, LANES)).reshape(2, 2, 2, BLOCKS, 1, LANES)
    units = jnp.concatenate([units[..., :ROW_C, :], c, units[..., ROW_C + 1 :, :]], axis=-2)
    for dim, axis in ((0, "gx"), (1, "gy"), (2, "gz")):
        low = lax.slice_in_dim(units, 0, 1, axis=dim)
        high = lax.slice_in_dim(units, 1, 2, axis=dim)
        c = slice(ROW_C, ROW_C + 1)
        far = from_last(
            jnp.concatenate([low[..., :5, :], high[..., c, :], low[..., ROW_C:, :]], axis=-2), axis
        )
        upper = low[..., dim : dim + 1, :] >= 0.5
        low_c = jnp.where(upper, low[..., c, :], far[..., 5:6, :])
        low = jnp.concatenate([low[..., :ROW_C, :], low_c, low[..., ROW_C + 1 :, :]], axis=-2)
        units = jnp.concatenate([far, low, high], axis=dim)
    dens, accel = run_force(
        units.reshape(27, BLOCKS, 8, LANES), hot, row(old_density), row(active)
    )
    return dens.reshape(1, 1, 1, COUNT), accel.reshape(1, 1, 1, 3, COUNT)


def solution(mesh):
    cells = P("gx", "gy", "gz", None)
    vectors = P("gx", "gy", "gz", None, None)
    return jax.shard_map(
        body,
        mesh=mesh,
        in_specs=(vectors, cells, cells, cells, cells, cells),
        out_specs=(cells, vectors),
        check_vma=False,
    )
```
